512 devices in a mesh: dp: 128 (over x, z, y_hi, core), rep: 4 (over y_lo).
Axes of the slice: x: 4, y: 8 (y_hi: 2, y_lo: 4; y = y_hi * 4 + y_lo), z: 8, core: 2. Of those that a mesh axis runs over, the one named last changes fastest.
Arguments:
- pooled_visual_vectors: bfloat16 [131072, 1152], P(('dp', 'rep')), may hold values from -4 to 4
- unnormalized_sentence_vectors: bfloat16 [131072, 1152], P(('dp', 'rep')), may hold values from -4 to 4
- projection_kernel: bfloat16 [1152, 1152], P('rep'), may hold values from -0.1875 to 0.1875
- matching_caption_index: int32 [131072], P(('dp', 'rep')), may hold values from 0 to 131071, as said below
- similarity_multiplier: float32 [1], replicated, may hold values from 5 to 15
- score_shift: float32 [1], replicated, may hold values from -3 to -1
Outputs:
- image_grad: bfloat16 [131072, 1152], P(('dp', 'rep'))
- text_grad: bfloat16 [131072, 1152], P(('dp', 'rep'))
- head_grad: float32 [1152, 1152], P('rep')
The draws below stay inside these ranges and needn't reach their ends.
Inputs may be any that keep to these rules, and one draw needn't show every extreme that they name: `matching_caption_index`: each image's matching text lies in its own block or in its partner block at distance 1 or 64.
All inputs are finite; a program needn't handle non-finite values.
Results may differ from the reference program's by a relative error of at most 0.0065.
Values may be sent and summed in bfloat16 or wider, within the bound.
A program may use at most 64 MiB of HBM per device.

```python
import math
import jax
import jax.numpy as jnp
from jax import lax

D = 1152
E = 1152
TOK_DEV = 256
TOKENS = 131072
N_DP = 128
N_REP = 4


def scaled_rows(key, row_count, col_count):
    key_base, key_row, key_col = jax.random.split(key, 3)
    base_vals = jnp.clip(jax.random.normal(key_base, (row_count, col_count), jnp.float32), -4.0, 4.0)
    row_scale = jnp.exp(jax.random.uniform(key_row, (row_count, 1), jnp.float32, 0.0, math.log(10.0)))
    col_scale = jnp.exp(jax.random.uniform(key_col, (1, col_count), jnp.float32, 0.0, math.log(10.0)))
    return base_vals * row_scale * col_scale * 0.01


def draw_pooled_visual_vectors(key, part):
    key = jax.random.fold_in(key, 11)
    return scaled_rows(key, TOKENS, D).astype(jnp.bfloat16)


def draw_unnormalized_sentence_vectors(key, part):
    key = jax.random.fold_in(key, 23)
    return scaled_rows(key, TOKENS, E).astype(jnp.bfloat16)


def draw_matching_caption_index(key, part):
    key = jax.random.fold_in(key, 37)
    key_section, key_offset = jax.random.split(key)
    row_index = jnp.arange(TOKENS, dtype=jnp.int32)
    block_index = row_index // TOK_DEV
    dp_place = block_index // N_REP
    rep_place = block_index % N_REP
    section_pick = jax.random.randint(key_section, (TOKENS,), 0, 3, dtype=jnp.int32)
    distance = jnp.where(section_pick == 0, 0, jnp.where(section_pick == 1, 1, N_DP // 2)).astype(jnp.int32)
    partner_block = jnp.bitwise_xor(dp_place, distance) * N_REP + rep_place
    offset_pick = jax.random.randint(key_offset, (TOKENS,), 0, TOK_DEV, dtype=jnp.int32)
    return (partner_block * TOK_DEV + offset_pick).astype(jnp.int32)


def shard_levels(own_key, shape, cuts, least, top_value):
    level = 1.0
    for position, shards_of in cuts:
        heights = jax.random.uniform(jax.random.fold_in(jax.random.fold_in(own_key, 6), position), (shards_of,), jnp.float32, least / len(cuts), top_value / len(cuts))
        level = level * jnp.repeat(jnp.exp(heights), shape[position] // shards_of).reshape((-1,) + (1,) * (len(shape) - 1 - position))
    return level


def gaussian(key, shape, scale, reach, cuts=(), kind=jnp.bfloat16):
    values = scale * jax.random.normal(key, shape, jnp.float32)
    if cuts:
        values = values * shard_levels(key, shape, cuts, -0.22, 0.18)
    return jnp.clip(values, -reach, reach).astype(kind)


def setup_inputs(seed: int = 0) -> dict:
    seeds = jax.random.split(jax.random.key(seed), 7)
    pooled_visual_vectors = draw_pooled_visual_vectors(jax.random.fold_in(seeds[6], 71), 0)
    unnormalized_sentence_vectors = draw_unnormalized_sentence_vectors(jax.random.fold_in(seeds[6], 71), 0)
    projection_kernel = gaussian(seeds[2], (D, E), D ** -0.5, 0.1875, ((0, 4),))
    matching_caption_index = draw_matching_caption_index(jax.random.fold_in(seeds[6], 71), 0)
    similarity_multiplier = jnp.clip(jax.random.uniform(seeds[4], (1,), jnp.float32, 5.0, 15.0), 5.0, 15.0)
    score_shift = jnp.clip(jax.random.uniform(seeds[5], (1,), jnp.float32, -3.0, -1.0), -3.0, -1.0)
    return {"pooled_visual_vectors": pooled_visual_vectors, "unnormalized_sentence_vectors": unnormalized_sentence_vectors, "projection_kernel": projection_kernel, "matching_caption_index": matching_caption_index, "similarity_multiplier": similarity_multiplier, "score_shift": score_shift}


epsilon = 1e-06

def unit_rows(raw_rows):
    norm_rows = jnp.sqrt(lax.optimization_barrier(jnp.sum(raw_rows * raw_rows, axis=-1, keepdims=True)) + epsilon)
    return (raw_rows / norm_rows, norm_rows)

def reference(pooled_visual_vectors, unnormalized_sentence_vectors, projection_kernel, matching_caption_index, similarity_multiplier, score_shift):
    smoothing_coefficient = similarity_multiplier[0]
    logit_offset_bias = score_shift[0]
    raw_image = jnp.dot(pooled_visual_vectors, projection_kernel, preferred_element_type=jnp.float32)
    image_unit, image_norm = unit_rows(raw_image)
    image_emb = lax.optimization_barrier(image_unit.astype(jnp.bfloat16))
    text_unit, text_norm = unit_rows(unnormalized_sentence_vectors.astype(jnp.float32))
    text_emb = lax.optimization_barrier(text_unit.astype(jnp.bfloat16))
    image_blocks = image_emb.reshape(N_DP, N_REP, TOK_DEV, E)
    text_blocks = text_emb.reshape(N_DP, N_REP, TOK_DEV, E)
    pair_blocks = matching_caption_index.reshape(N_DP, N_REP, TOK_DEV)
    global_ids = jnp.arange(TOKENS, dtype=jnp.int32).reshape(N_DP, N_REP, TOK_DEV)

    def section_block(operands):
        image_part, text_part, pair_part, id_part = operands
        image_broad_rows = image_part.astype(jnp.float32)
        text_broad_rows = text_part.astype(jnp.float32)
        logit_matrix = smoothing_coefficient * jnp.einsum('gjy,gdy->gjd', image_broad_rows, text_broad_rows) + logit_offset_bias
        label = jnp.where(pair_part[:, :, None] == id_part[:, None, :], 1.0, -1.0).astype(jnp.float32)
        weight_matrix = lax.optimization_barrier((-label * jax.nn.sigmoid(-label * logit_matrix)).astype(jnp.bfloat16))
        weight_broad_matrix = weight_matrix.astype(jnp.float32)
        image_piece_direction = smoothing_coefficient * jnp.einsum('hza,han->hzn', weight_broad_matrix, text_broad_rows)
        text_piece_direction = smoothing_coefficient * jnp.einsum('hfm,hfj->hmj', weight_broad_matrix, image_broad_rows)
        return (image_piece_direction, text_piece_direction)
    image_dir = jnp.zeros((N_DP, N_REP, TOK_DEV, E), jnp.float32)
    text_dir = jnp.zeros((N_DP, N_REP, TOK_DEV, E), jnp.float32)
    for distance in [0, 1, N_DP // 2]:
        partner = jnp.bitwise_xor(jnp.arange(N_DP, dtype=jnp.int32), jnp.int32(distance))
        image_terms, text_terms = lax.map(section_block, (image_blocks, text_blocks[partner], pair_blocks, global_ids[partner]))
        image_dir = image_dir + image_terms
        if distance == 0:
            text_dir = text_dir + text_terms
        else:
            rounded = lax.optimization_barrier(text_terms.astype(jnp.bfloat16))
            text_dir = text_dir + rounded.astype(jnp.float32)[partner]
    image_dir = image_dir.reshape(TOKENS, E)
    text_dir = text_dir.reshape(TOKENS, E)
    image_back = ((image_dir - image_unit * lax.optimization_barrier(jnp.sum(image_unit * image_dir, axis=-1, keepdims=True))) / image_norm).astype(jnp.bfloat16)
    image_grad = jnp.dot(image_back, projection_kernel.T, preferred_element_type=jnp.float32).astype(jnp.bfloat16)
    text_grad = ((text_dir - text_unit * lax.optimization_barrier(jnp.sum(text_unit * text_dir, axis=-1, keepdims=True))) / text_norm).astype(jnp.bfloat16)
    head_grad = jnp.dot(pooled_visual_vectors.T, image_back, preferred_element_type=jnp.float32)
    return (image_grad, text_grad, head_grad)
```

```python
import functools

import jax
import jax.numpy as jnp
from jax import lax
from jax.experimental import pallas as pl
from jax.experimental.pallas import tpu as pltpu
from jax.sharding import PartitionSpec as P

EPS = 1e-06
BF = jnp.bfloat16
F32 = jnp.float32
MESH = pl.DeviceIdType.MESH

NX, NY, NZ = 4, 8, 8
REP = 4
TOK = 256
DIM = 1152
LANE = 128
COLS = DIM // LANE
SHARD = DIM // REP
HALF = SHARD // 2
NTILE = 384

A_X = 240
A_LAST = 672
A_ROWS = 912
A_Z = 32
A_ZLAST = 208
B_Z = 48
B_X = 16
B_XN = 3


def coords():
    dp = lax.axis_index("dp")
    rep = lax.axis_index("rep")
    core = lax.rem(dp, 2)
    y_hi = lax.rem(dp // 2, 2)
    z = lax.rem(dp // 4, NZ)
    x = dp // 32
    return x, y_hi * REP + rep, z, core


def device(x, y, z, core):
    return (((x * NZ + z) * 2 + y // REP) * 2 + core, lax.rem(y, REP))


def remote(src, dst, send_sem, recv_sem, to):
    return pltpu.make_async_remote_copy(
        src_ref=src,
        dst_ref=dst,
        send_sem=send_sem,
        recv_sem=recv_sem,
        device_id=to,
        device_id_type=MESH,
    )


def each(count, step):
    def run(k, carry):
        step(k)
        return carry

    lax.fori_loop(1, count, run, 0)


def rows_of(total, step, size=32):
    def run(i, carry):
        step(pl.ds(pl.multiple_of(i * size, size), size))
        return carry

    lax.fori_loop(0, total // size, run, 0)


def mm(a, b):
    return jnp.dot(a, b, preferred_element_type=F32)


def mm_nt(a, b):
    return lax.dot_general(a, b, (((1,), (1,)), ((), ())), preferred_element_type=F32)


def sigmoid_weight(logits, match):
    value = jax.nn.sigmoid(jnp.where(match, -logits, logits))
    return jnp.where(match, -value, value).astype(BF)


def kernel(
    pooled_in,
    text_in,
    head_in,
    idx_in,
    mult_ref,
    shift_ref,
    image_out,
    text_out,
    head_out,
    pooled,
    text_raw,
    text_emb,
    idx,
    idx_rows,
    head,
    pooled_t,
    pooled_sel,
    raw,
    norm,
    text_norm,
    image_emb,
    weight,
    direction,
    back,
    part,
    recv_ax,
    sum_ax,
    recv_az,
    recv_bz,
    sum_bz,
    recv_bx,
    mid,
    recv_y,
    done,
    gather_az,
    gather_bx,
    full_a,
    full_b,
    image_stage,
    text_stage,
    head_stage,
    loc_sem,
    swap_send,
    swap_recv,
    far_send,
    far_recv,
    head_send,
    head_recv,
    fwd_send,
    fwd_recv,
    back_send,
    back_recv,
    ax_send,
    ax_recv,
    bz_send,
    bz_recv,
    az_send,
    az_recv,
    bx_send,
    bx_recv,
    y_send,
    y_recv,
    ga_send,
    ga_recv,
    gb_send,
    gb_recv,
    fa_send,
    fa_recv,
    fb_send,
    fb_recv,
    end_send,
    end_recv,
):
    x, y, z, core = coords()
    rep = lax.rem(y, REP)
    other = device(x, y, z, 1 - core)

    def at_x(k):
        return device(lax.rem(x + k, NX), y, z, core)

    def at_y(k):
        return device(x, lax.rem(y + k, NY), z, core)

    def at_z(k):
        return device(x, y, lax.rem(z + k, NZ), core)

    far = at_x(2)

    own = pl.ds(0, TOK)
    sib = pl.ds(TOK, TOK)
    off = pl.ds(2 * TOK, TOK)
    shard_at = pl.multiple_of(rep * SHARD, 16)
    local = [
        pltpu.make_async_copy(text_in, text_raw.at[own], loc_sem.at[0]),
        pltpu.make_async_copy(pooled_in, pooled.at[own], loc_sem.at[1]),
        pltpu.make_async_copy(idx_in, idx.at[0], loc_sem.at[2]),
        pltpu.make_async_copy(head_in, head.at[pl.ds(shard_at, SHARD)], loc_sem.at[3]),
    ]
    for copy in local:
        copy.start()

    barrier = pltpu.get_barrier_semaphore()
    pl.semaphore_signal(barrier, inc=1, device_id=other, device_id_type=MESH)
    for count, at in ((NX, at_x), (NY, at_y), (NZ, at_z)):
        each(
            count,
            lambda k, at=at: pl.semaphore_signal(
                barrier, inc=1, device_id=at(k), device_id_type=MESH
            ),
        )
    pl.semaphore_wait(barrier, 1 + (NX - 1) + (NY - 1) + (NZ - 1))

    half_at = pl.multiple_of(core * HALF, 16)
    mine_at = pl.multiple_of(rep * SHARD + core * HALF, 16)
    long, short = 80, 64
    head_copies = [
        remote(
            head_in.at[pl.ds(half_at, HALF)],
            head.at[pl.ds(mine_at, HALF)],
            head_send.at[0],
            head_recv.at[0],
            at_y(1),
        ),
        remote(
            head_in.at[pl.ds(half_at, HALF)],
            head.at[pl.ds(mine_at, HALF)],
            head_send.at[1],
            head_recv.at[1],
            at_y(NY - 1),
        ),
        remote(
            head_in.at[pl.ds(half_at, long)],
            head.at[pl.ds(mine_at, long)],
            head_send.at[2],
            head_recv.at[2],
            at_y(2),
        ),
        remote(
            head_in.at[pl.ds(pl.multiple_of(half_at + long, 16), short)],
            head.at[pl.ds(pl.multiple_of(mine_at + long, 16), short)],
            head_send.at[3],
            head_recv.at[3],
            at_y(NY - 2),
        ),
    ]
    far_text = remote(text_in, text_raw.at[off], far_send.at[0], far_recv.at[0], far)
    far_idx = remote(idx_in, idx.at[2], far_send.at[1], far_recv.at[1], far)
    far_pooled = remote(pooled_in, pooled.at[off], far_send.at[2], far_recv.at[2], far)
    swaps = [
        remote(text_in, text_raw.at[sib], swap_send.at[0], swap_recv.at[0], other),
        remote(pooled_in, pooled.at[sib], swap_send.at[1], swap_recv.at[1], other),
        remote(idx_in, idx.at[1], swap_send.at[2], swap_recv.at[2], other),
    ]
    far_text.start()
    for copy in head_copies:
        copy.start()
    far_idx.start()
    for copy in swaps:
        copy.start()

    scale = mult_ref[0]
    shift = shift_ref[0]

    def text_rows(start):
        def step(block):
            rows = pl.ds(pl.multiple_of(start + block.start, 32), 32)
            value = text_raw[rows, :].astype(F32)
            inverse = 1.0 / jnp.sqrt(jnp.sum(value * value, axis=-1, keepdims=True) + EPS)
            text_emb[rows, :] = (value * inverse).astype(BF)
            if start == 0:
                text_norm[block, :] = inverse

        rows_of(TOK, step)

    def turn(start):
        for j in range(COLS):
            cols = pl.ds(j * LANE, LANE)
            pooled_t[cols, pl.ds(start, TOK)] = pooled[pl.ds(start, TOK), cols].T

    local[0].wait()
    text_rows(0)
    local[1].wait()
    local[2].wait()
    turn(0)
    idx_rows[...] = jnp.broadcast_to(idx[0].astype(F32), (TOK, TOK)).T
    for copy in swaps:
        copy.wait_recv()
    text_rows(TOK)
    turn(TOK)
    for q in range(REP):
        pooled_sel[pl.ds(q * HALF, HALF), :] = pooled_t[
            pl.ds(pl.multiple_of(q * SHARD + core * HALF, 16), HALF), :
        ]
    local[3].wait()

    def forward(slot, shift_y, begin, count):
        at = pl.multiple_of(
            lax.rem(y + NY - shift_y, REP) * SHARD + core * HALF + begin, 16
        )
        rows = pl.ds(at, count)
        copy = remote(head.at[rows], head.at[rows], fwd_send.at[slot], fwd_recv.at[slot], other)
        copy.start()
        return copy

    head_copies[0].wait_recv()
    forwards = [forward(0, 1, 0, HALF)]
    head_copies[1].wait_recv()
    forwards.append(forward(1, NY - 1, 0, HALF))
    head_copies[2].wait_recv()
    forwards.append(forward(2, 2, 0, long))
    head_copies[3].wait_recv()
    forwards.append(forward(3, NY - 2, long, short))

    far_text.wait_recv()
    far_idx.wait_recv()
    far_pooled.start()
    text_rows(2 * TOK)
    for copy in forwards:
        copy.wait_recv()

    for j in range(DIM // NTILE):
        cols = pl.ds(j * NTILE, NTILE)
        raw[:, cols] = mm(pooled[own, :], head[:, cols])

    def image_rows(block):
        value = raw[block, :]
        inverse = 1.0 / jnp.sqrt(jnp.sum(value * value, axis=-1, keepdims=True) + EPS)
        unit = value * inverse
        raw[block, :] = unit
        norm[block, :] = inverse
        image_emb[block, :] = unit.astype(BF)

    rows_of(TOK, image_rows)

    dp = lax.axis_index("dp")
    dp_other = dp + 1 - 2 * core
    dp_far = lax.rem(dp + 64, 128)
    lane_id = lax.broadcasted_iota(jnp.int32, (TOK, TOK), 1).astype(F32)
    row_id = lax.broadcasted_iota(jnp.int32, (TOK, TOK), 0).astype(F32)
    own_base = ((dp * REP + rep) * TOK).astype(F32)
    for j, place in enumerate((dp, dp_other, dp_far)):
        base = ((place * REP + rep) * TOK).astype(F32)
        rows = pl.ds(j * TOK, TOK)
        logits = scale * mm_nt(image_emb[own, :], text_emb[rows, :]) + shift
        weight[:, rows] = sigmoid_weight(logits, idx_rows[...] == lane_id + base)

    for j in range(DIM // NTILE):
        cols = pl.ds(j * NTILE, NTILE)
        direction[:, cols] = scale * mm(weight[...], text_emb[:, cols])

    def back_rows(block):
        unit = raw[block, :]
        value = direction[block, :]
        inner = jnp.sum(unit * value, axis=-1, keepdims=True)
        back[block, :] = ((value - unit * inner) * norm[block, :]).astype(BF)

    rows_of(TOK, back_rows)
    back_copy = remote(back.at[own], back.at[sib], back_send.at[0], back_recv.at[0], other)
    back_copy.start()
    back_copy.wait_recv()

    for first, width in ((0, 256), (256, 256), (512, 256), (768, 256), (1024, 128)):
        value = mm(pooled_sel[...], back[:, pl.ds(first, width)]).astype(BF)
        for jj in range(width // LANE):
            j = first // LANE + jj
            for q in range(REP):
                part[q, pl.ds(j * HALF, HALF), :] = value[
                    q * HALF : (q + 1) * HALF, jj * LANE : (jj + 1) * LANE
                ]

    def a_start(place):
        return pl.multiple_of(jnp.minimum(place * A_X, A_LAST), 16)

    def az_start(place):
        return pl.multiple_of(jnp.minimum(place * A_Z, A_ZLAST), 16)

    def b_start(place):
        return pl.multiple_of(A_ROWS + place * B_Z, 16)

    def bx_start(place):
        return pl.multiple_of(jnp.minimum(place, B_XN - 1) * B_X, 16)

    def ax_copy(k):
        src = part.at[:, pl.ds(a_start(lax.rem(x + k, NX)), A_X), :]
        return remote(src, recv_ax.at[k], ax_send.at[k], ax_recv.at[k], at_x(k))

    def bz_copy(k):
        src = part.at[:, pl.ds(b_start(lax.rem(z + k, NZ)), B_Z), :]
        return remote(src, recv_bz.at[k], bz_send.at[k], bz_recv.at[k], at_z(k))

    def az_copy(k):
        src = sum_ax.at[:, pl.ds(az_start(lax.rem(z + k, NZ)), A_Z), :]
        return remote(src, recv_az.at[k], az_send.at[k], az_recv.at[k], at_z(k))

    def bx_copy(k):
        src = sum_bz.at[:, pl.ds(bx_start(lax.rem(x + k, NX)), B_X), :]
        return remote(src, recv_bx.at[k], bx_send.at[k], bx_recv.at[k], at_x(k))

    def y_copy(k):
        src = mid.at[lax.rem(y + k, REP)]
        return remote(src, recv_y.at[y], y_send.at[k], y_recv.at[k], at_y(k))

    def ga_copy(k):
        src = done.at[pl.ds(0, A_Z)]
        return remote(src, gather_az.at[z], ga_send.at[k], ga_recv.at[k], at_z(k))

    def gb_copy(k):
        src = done.at[pl.ds(A_Z, B_X)]
        return remote(src, gather_bx.at[x], gb_send.at[k], gb_recv.at[k], at_x(k))

    def fa_copy(k):
        return remote(gather_az, full_a.at[core, x], fa_send.at[k], fa_recv.at[k], at_x(k))

    def fb_copy(k):
        return remote(gather_bx, full_b.at[core, z], fb_send.at[k], fb_recv.at[k], at_z(k))

    each(NX, lambda k: ax_copy(k).start())
    each(NZ, lambda k: bz_copy(k).start())

    for j in range(DIM // NTILE):
        cols = pl.ds(j * NTILE, NTILE)
        image_stage[:, cols] = mm_nt(back[own, :], head[cols, :]).astype(BF)
    image_save = pltpu.make_async_copy(image_stage, image_out, loc_sem.at[4])
    image_save.start()

    far_pooled.wait_recv()
    for i in (1, 2):
        part_rows = pl.ds(i * TOK, TOK)
        for j in range(DIM // NTILE):
            cols = pl.ds(j * NTILE, NTILE)
            direction[:, cols] = mm(pooled[part_rows, :], head[:, cols])

        def emb_rows(block):
            value = direction[block, :]
            inverse = 1.0 / jnp.sqrt(jnp.sum(value * value, axis=-1, keepdims=True) + EPS)
            rows = pl.ds(pl.multiple_of(i * TOK + block.start, 32), 32)
            image_emb[rows, :] = (value * inverse).astype(BF)

        rows_of(TOK, emb_rows)

    for j in range(3):
        rows = pl.ds(j * TOK, TOK)
        logits = scale * mm_nt(text_emb[own, :], image_emb[rows, :]) + shift
        match = idx[j].astype(F32) == row_id + own_base
        weight[:, rows] = sigmoid_weight(logits, match)
    for j in range(DIM // NTILE):
        cols = pl.ds(j * NTILE, NTILE)
        direction[:, cols] = scale * mm(weight[...], image_emb[:, cols])

    def text_back(block):
        inverse = text_norm[block, :]
        unit = text_raw[block, :].astype(F32) * inverse
        value = direction[block, :]
        inner = jnp.sum(unit * value, axis=-1, keepdims=True)
        text_stage[block, :] = ((value - unit * inner) * inverse).astype(BF)

    rows_of(TOK, text_back)
    text_save = pltpu.make_async_copy(text_stage, text_out, loc_sem.at[5])
    text_save.start()

    each(NX, lambda k: ax_copy(k).wait_recv())
    own_at = a_start(x)
    for q in range(REP):
        total = part[q, pl.ds(own_at, A_X), :].astype(F32)
        for k in range(1, NX):
            total = total + recv_ax[k, q].astype(F32)
        sum_ax[q] = total.astype(BF)
    each(NZ, lambda k: az_copy(k).start())
    each(NZ, lambda k: bz_copy(k).wait_recv())
    own_at = b_start(z)
    for q in range(REP):
        total = part[q, pl.ds(own_at, B_Z), :].astype(F32)
        for k in range(1, NZ):
            total = total + recv_bz[k, q].astype(F32)
        sum_bz[q] = total.astype(BF)
    each(NX, lambda k: bx_copy(k).start())

    each(NX, lambda k: bx_copy(k).wait_recv())
    total = sum_bz[:, pl.ds(bx_start(x), B_X), :].astype(F32)
    for k in range(1, NX):
        total = total + recv_bx[k].astype(F32)
    mid[:, pl.ds(A_Z, B_X), :] = total.astype(BF)
    each(NZ, lambda k: az_copy(k).wait_recv())
    total = sum_ax[:, pl.ds(az_start(z), A_Z), :].astype(F32)
    for k in range(1, NZ):
        total = total + recv_az[k].astype(F32)
    mid[:, pl.ds(0, A_Z), :] = total.astype(BF)

    each(NY, lambda k: y_copy(k).start())
    recv_y[y] = mid[rep]
    each(NY, lambda k: y_copy(k).wait_recv())
    total = recv_y[0].astype(F32)
    for k in range(1, NY):
        total = total + recv_y[k].astype(F32)
    done[...] = total.astype(BF)

    each(NX, lambda k: gb_copy(k).start())
    each(NZ, lambda k: ga_copy(k).start())
    gather_bx[x] = done[pl.ds(A_Z, B_X), :]
    gather_az[z] = done[pl.ds(0, A_Z), :]
    each(NX, lambda k: gb_copy(k).wait_recv())
    each(NZ, lambda k: fb_copy(k).start())
    each(NZ, lambda k: ga_copy(k).wait_recv())
    each(NX, lambda k: fa_copy(k).start())
    full_b[core, z] = gather_bx[...]
    full_a[core, x] = gather_az[...]
    each(NX, lambda k: fa_copy(k).wait_recv())
    each(NZ, lambda k: fb_copy(k).wait_recv())
    end_copies = [
        remote(full_a.at[core], full_a.at[core], end_send.at[0], end_recv.at[0], other),
        remote(full_b.at[core], full_b.at[core], end_send.at[1], end_recv.at[1], other),
    ]
    for copy in end_copies:
        copy.start()
    for copy in end_copies:
        copy.wait_recv()

    for half in range(2):
        for tile in range(COLS * 9):
            j, row = tile // 9, tile % 9
            if tile < A_ROWS // 16:
                place = min(tile // 15, NX - 1)
                rest = tile - min(place * 15, A_LAST // 16)
                piece = min(rest // 2, NZ - 1)
                at = rest - min(piece * 2, A_ZLAST // 16)
                value = full_a[half, place, piece, pl.ds(at * 16, 16), :]
            else:
                rest = tile - A_ROWS // 16
                value = full_b[half, rest // 3, rest % 3]
            head_stage[pl.ds(half * HALF + row * 16, 16), pl.ds(j * LANE, LANE)] = value
    head_save = pltpu.make_async_copy(head_stage, head_out, loc_sem.at[6])
    head_save.start()

    far_text.wait_send()
    far_idx.wait_send()
    far_pooled.wait_send()
    for copy in head_copies + swaps + forwards + [back_copy] + end_copies:
        copy.wait_send()
    for count, copy in (
        (NX, ax_copy),
        (NZ, bz_copy),
        (NZ, az_copy),
        (NX, bx_copy),
        (NY, y_copy),
        (NZ, ga_copy),
        (NX, gb_copy),
        (NX, fa_copy),
        (NZ, fb_copy),
    ):
        each(count, lambda k, copy=copy: copy(k).wait_send())
    image_save.wait()
    text_save.wait()
    head_save.wait()


def body(pooled, text, head, idx, mult, shift):
    dma = pltpu.SemaphoreType.DMA
    vmem = pltpu.VMEM
    scratch = [
        vmem((3 * TOK, DIM), BF),
        vmem((3 * TOK, DIM), BF),
        vmem((3 * TOK, DIM), BF),
        vmem((3, 1, TOK), jnp.int32),
        vmem((TOK, TOK), F32),
        vmem((DIM, DIM), BF),
        vmem((DIM, 2 * TOK), BF),
        vmem((REP * HALF, 2 * TOK), BF),
        vmem((TOK, DIM), F32),
        vmem((TOK, 1), F32),
        vmem((TOK, 1), F32),
        vmem((3 * TOK, DIM), BF),
        vmem((TOK, 3 * TOK), BF),
        vmem((TOK, DIM), F32),
        vmem((2 * TOK, DIM), BF),
        vmem((REP, COLS * HALF, LANE), BF),
        vmem((NX, REP, A_X, LANE), BF),
        vmem((REP, A_X, LANE), BF),
        vmem((NZ, REP, A_Z, LANE), BF),
        vmem((NZ, REP, B_Z, LANE), BF),
        vmem((REP, B_Z, LANE), BF),
        vmem((NX, REP, B_X, LANE), BF),
        vmem((REP, A_Z + B_X, LANE), BF),
        vmem((NY, A_Z + B_X, LANE), BF),
        vmem((A_Z + B_X, LANE), BF),
        vmem((NZ, A_Z, LANE), BF),
        vmem((NX, B_X, LANE), BF),
        vmem((2, NX, NZ, A_Z, LANE), BF),
        vmem((2, NZ, NX, B_X, LANE), BF),
        vmem((TOK, DIM), BF),
        vmem((TOK, DIM), BF),
        vmem((SHARD, DIM), BF),
        dma((7,)),
    ]
    for count in (3, 3, 4, 4, 1, NX, NZ, NZ, NX, NY, NZ, NX, NX, NZ, 2):
        scratch += [dma((count,)), dma((count,))]
    hbm = pl.BlockSpec(memory_space=pl.ANY)
    smem = pl.BlockSpec(memory_space=pltpu.SMEM)
    image_grad, text_grad, head_grad = pl.pallas_call(
        kernel,
        out_shape=(
            jax.ShapeDtypeStruct((TOK, DIM), BF),
            jax.ShapeDtypeStruct((TOK, DIM), BF),
            jax.ShapeDtypeStruct((SHARD, DIM), BF),
        ),
        in_specs=[hbm, hbm, hbm, hbm, smem, smem],
        out_specs=(hbm, hbm, hbm),
        scratch_shapes=scratch,
        compiler_params=pltpu.CompilerParams(
            collective_id=0, has_side_effects=True, vmem_limit_bytes=56 * 2**20
        ),
        name="contrastive",
    )(pooled, text, head, idx.reshape(1, TOK), mult, shift)
    return image_grad, text_grad, head_grad.astype(F32)


def solution(mesh):
    rows = P(("dp", "rep"), None)
    in_specs = (rows, rows, P("rep", None), P(("dp", "rep")), P(), P())
    out_specs = (rows, rows, P("rep", None))
    return jax.shard_map(body, mesh=mesh, in_specs=in_specs, out_specs=out_specs, check_vma=False)
```

```python
import functools

import jax
import jax.numpy as jnp
from jax import lax
from jax.experimental import pallas as pl
from jax.experimental.pallas import tpu as pltpu
from jax.sharding import PartitionSpec as P

EPS = 1e-06
BF = jnp.bfloat16
F32 = jnp.float32
MESH = pl.DeviceIdType.MESH

NX, NY, NZ = 4, 8, 8
REP = 4
TOK = 256
DIM = 1152
LANE = 128
COLS = DIM // LANE
SHARD = DIM // REP
HALF = SHARD // 2
NTILE = 384
GROUP = 2

A_X = 240
A_LAST = 672
A_ROWS = 912
A_Z = 32
A_ZLAST = 208
B_Z = 48
B_X = 16
B_XN = 3


def coords():
    dp = lax.axis_index("dp")
    rep = lax.axis_index("rep")
    core = lax.rem(dp, 2)
    y_hi = lax.rem(dp // 2, 2)
    z = lax.rem(dp // 4, NZ)
    x = dp // 32
    return x, y_hi * REP + rep, z, core


def device(x, y, z, core):
    return (((x * NZ + z) * 2 + y // REP) * 2 + core, lax.rem(y, REP))


def remote(src, dst, send_sem, recv_sem, to):
    return pltpu.make_async_remote_copy(
        src_ref=src,
        dst_ref=dst,
        send_sem=send_sem,
        recv_sem=recv_sem,
        device_id=to,
        device_id_type=MESH,
    )


def each(count, step):
    def run(k, carry):
        step(k)
        return carry

    lax.fori_loop(1, count, run, 0)


def rows_of(total, step, size=32):
    def run(i, carry):
        step(pl.ds(pl.multiple_of(i * size, size), size))
        return carry

    lax.fori_loop(0, total // size, run, 0)


def mm(a, b):
    return jnp.dot(a, b, preferred_element_type=F32)


def mm_nt(a, b):
    return lax.dot_general(a, b, (((1,), (1,)), ((), ())), preferred_element_type=F32)


def sigmoid_weight(logits, match):
    value = jax.nn.sigmoid(jnp.where(match, -logits, logits))
    return jnp.where(match, -value, value).astype(BF)


def kernel(
    pooled_in,
    text_in,
    head_in,
    idx_in,
    mult_ref,
    shift_ref,
    image_out,
    text_out,
    head_out,
    pooled,
    text_raw,
    text_emb,
    idx,
    idx_rows,
    head,
    pooled_t,
    pooled_sel,
    raw,
    norm,
    text_norm,
    image_emb,
    weight,
    direction,
    back,
    part,
    recv_ax,
    sum_ax,
    recv_az,
    recv_bz,
    sum_bz,
    recv_bx,
    mid,
    recv_y,
    done,
    gather_az,
    gather_bx,
    full_a,
    full_b,
    image_stage,
    text_stage,
    head_stage,
    loc_sem,
    swap_send,
    swap_recv,
    far_send,
    far_recv,
    head_send,
    head_recv,
    fwd_send,
    fwd_recv,
    back_send,
    back_recv,
    ax_send,
    ax_recv,
    bz_send,
    bz_recv,
    az_send,
    az_recv,
    bx_send,
    bx_recv,
    y_send,
    y_recv,
    ga_send,
    ga_recv,
    gb_send,
    gb_recv,
    fa_send,
    fa_recv,
    fb_send,
    fb_recv,
    end_send,
    end_recv,
):
    x, y, z, core = coords()
    rep = lax.rem(y, REP)
    other = device(x, y, z, 1 - core)

    def at_x(k):
        return device(lax.rem(x + k, NX), y, z, core)

    def at_y(k):
        return device(x, lax.rem(y + k, NY), z, core)

    def at_z(k):
        return device(x, y, lax.rem(z + k, NZ), core)

    far = at_x(2)

    own = pl.ds(0, TOK)
    sib = pl.ds(TOK, TOK)
    off = pl.ds(2 * TOK, TOK)
    shard_at = pl.multiple_of(rep * SHARD, 16)
    local = [
        pltpu.make_async_copy(text_in, text_raw.at[own], loc_sem.at[0]),
        pltpu.make_async_copy(pooled_in, pooled.at[own], loc_sem.at[1]),
        pltpu.make_async_copy(idx_in, idx.at[0], loc_sem.at[2]),
        pltpu.make_async_copy(head_in, head.at[pl.ds(shard_at, SHARD)], loc_sem.at[3]),
    ]
    for copy in local:
        copy.start()

    barrier = pltpu.get_barrier_semaphore()
    pl.semaphore_signal(barrier, inc=1, device_id=other, device_id_type=MESH)
    for count, at in ((NX, at_x), (NY, at_y), (NZ, at_z)):
        each(
            count,
            lambda k, at=at: pl.semaphore_signal(
                barrier, inc=1, device_id=at(k), device_id_type=MESH
            ),
        )
    pl.semaphore_wait(barrier, 1 + (NX - 1) + (NY - 1) + (NZ - 1))

    half_at = pl.multiple_of(core * HALF, 16)
    mine_at = pl.multiple_of(rep * SHARD + core * HALF, 16)
    long, short = 80, 64
    pieces = ((0, long, 1), (long, short, NY - 1), (long, short, 1), (0, long, NY - 1))
    head_copies = []
    for slot, (begin, count, step_y) in enumerate(pieces):
        head_copies.append(
            remote(
                head_in.at[pl.ds(pl.multiple_of(half_at + begin, 16), count)],
                head.at[pl.ds(pl.multiple_of(mine_at + begin, 16), count)],
                head_send.at[slot],
                head_recv.at[slot],
                at_y(step_y),
            )
        )
    far_text = remote(text_in, text_raw.at[off], far_send.at[0], far_recv.at[0], far)
    far_idx = remote(idx_in, idx.at[2], far_send.at[1], far_recv.at[1], far)
    far_pooled = remote(pooled_in, pooled.at[off], far_send.at[2], far_recv.at[2], far)
    swaps = [
        remote(text_in, text_raw.at[sib], swap_send.at[0], swap_recv.at[0], other),
        remote(pooled_in, pooled.at[sib], swap_send.at[1], swap_recv.at[1], other),
        remote(idx_in, idx.at[1], swap_send.at[2], swap_recv.at[2], other),
    ]
    far_text.start()
    for copy in head_copies:
        copy.start()
    far_idx.start()
    for copy in swaps:
        copy.start()

    scale = mult_ref[0]
    shift = shift_ref[0]

    def text_rows(start):
        def step(block):
            rows = pl.ds(pl.multiple_of(start + block.start, 32), 32)
            value = text_raw[rows, :].astype(F32)
            inverse = 1.0 / jnp.sqrt(jnp.sum(value * value, axis=-1, keepdims=True) + EPS)
            text_emb[rows, :] = (value * inverse).astype(BF)
            if start == 0:
                text_norm[block, :] = inverse

        rows_of(TOK, step)

    def turn(start):
        for j in range(COLS):
            cols = pl.ds(j * LANE, LANE)
            pooled_t[cols, pl.ds(start, TOK)] = pooled[pl.ds(start, TOK), cols].T

    local[0].wait()
    text_rows(0)
    local[1].wait()
    local[2].wait()
    turn(0)
    idx_rows[...] = jnp.broadcast_to(idx[0].astype(F32), (TOK, TOK)).T
    for copy in swaps:
        copy.wait_recv()
    text_rows(TOK)
    turn(TOK)
    for q in range(REP):
        pooled_sel[pl.ds(q * HALF, HALF), :] = pooled_t[
            pl.ds(pl.multiple_of(q * SHARD + core * HALF, 16), HALF), :
        ]
    local[3].wait()

    def rows_from(shift_y, begin, count):
        place = lax.rem(y + 2 * NY - shift_y, REP)
        return head.at[pl.ds(pl.multiple_of(place * SHARD + core * HALF + begin, 16), count)]

    forwards = []

    def forward(rows):
        slot = len(forwards)
        copy = remote(rows, rows, fwd_send.at[slot], fwd_recv.at[slot], other)
        copy.start()
        forwards.append(copy)

    relays = []
    for slot, (begin, count, step_y) in enumerate(pieces):
        head_copies[slot].wait_recv()
        rows = rows_from(step_y, begin, count)
        if slot < 2:
            relay = remote(rows, rows, head_send.at[4 + slot], head_recv.at[4 + slot], at_y(step_y))
            relay.start()
            relays.append(relay)
        forward(rows)
    for slot, (begin, count, step_y) in enumerate(pieces[:2]):
        relays[slot].wait_recv()
        forward(rows_from(2 * step_y, begin, count))

    far_text.wait_recv()
    far_pooled.start()
    far_idx.wait_recv()
    text_rows(2 * TOK)
    for copy in forwards:
        copy.wait_recv()

    for j in range(DIM // NTILE):
        cols = pl.ds(j * NTILE, NTILE)
        raw[:, cols] = mm(pooled[own, :], head[:, cols])

    def image_rows(block):
        value = raw[block, :]
        inverse = 1.0 / jnp.sqrt(jnp.sum(value * value, axis=-1, keepdims=True) + EPS)
        unit = value * inverse
        raw[block, :] = unit
        norm[block, :] = inverse
        image_emb[block, :] = unit.astype(BF)

    rows_of(TOK, image_rows)

    dp = lax.axis_index("dp")
    dp_other = dp + 1 - 2 * core
    dp_far = lax.rem(dp + 64, 128)
    lane_id = lax.broadcasted_iota(jnp.int32, (TOK, TOK), 1).astype(F32)
    row_id = lax.broadcasted_iota(jnp.int32, (TOK, TOK), 0).astype(F32)
    own_base = ((dp * REP + rep) * TOK).astype(F32)
    for j, place in enumerate((dp, dp_other, dp_far)):
        base = ((place * REP + rep) * TOK).astype(F32)
        rows = pl.ds(j * TOK, TOK)
        logits = scale * mm_nt(image_emb[own, :], text_emb[rows, :]) + shift
        weight[:, rows] = sigmoid_weight(logits, idx_rows[...] == lane_id + base)

    for j in range(DIM // NTILE):
        cols = pl.ds(j * NTILE, NTILE)
        direction[:, cols] = scale * mm(weight[...], text_emb[:, cols])

    def back_rows(block):
        unit = raw[block, :]
        value = direction[block, :]
        inner = jnp.sum(unit * value, axis=-1, keepdims=True)
        back[block, :] = ((value - unit * inner) * norm[block, :]).astype(BF)

    rows_of(TOK, back_rows)
    back_copy = remote(back.at[own], back.at[sib], back_send.at[0], back_recv.at[0], other)
    back_copy.start()
    back_copy.wait_recv()

    def rows_in(group):
        return pl.ds(group * GROUP, GROUP)

    def a_start(place):
        return pl.multiple_of(jnp.minimum(place * A_X, A_LAST), 16)

    def az_start(place):
        return pl.multiple_of(jnp.minimum(place * A_Z, A_ZLAST), 16)

    def b_start(place):
        return pl.multiple_of(A_ROWS + place * B_Z, 16)

    def bx_start(place):
        return pl.multiple_of(jnp.minimum(place, B_XN - 1) * B_X, 16)

    def ax_copy(group, k):
        src = part.at[rows_in(group), pl.ds(a_start(lax.rem(x + k, NX)), A_X), :]
        slot = group * NX + k
        dst = recv_ax.at[k, rows_in(group)]
        return remote(src, dst, ax_send.at[slot], ax_recv.at[slot], at_x(k))

    def bz_copy(group, k):
        src = part.at[rows_in(group), pl.ds(b_start(lax.rem(z + k, NZ)), B_Z), :]
        slot = group * NZ + k
        dst = recv_bz.at[k, rows_in(group)]
        return remote(src, dst, bz_send.at[slot], bz_recv.at[slot], at_z(k))

    def az_copy(group, k):
        src = sum_ax.at[rows_in(group), pl.ds(az_start(lax.rem(z + k, NZ)), A_Z), :]
        slot = group * NZ + k
        dst = recv_az.at[k, rows_in(group)]
        return remote(src, dst, az_send.at[slot], az_recv.at[slot], at_z(k))

    def bx_copy(group, k):
        src = sum_bz.at[rows_in(group), pl.ds(bx_start(lax.rem(x + k, NX)), B_X), :]
        slot = group * NX + k
        dst = recv_bx.at[k, rows_in(group)]
        return remote(src, dst, bx_send.at[slot], bx_recv.at[slot], at_x(k))

    def y_copy(k):
        to = lax.rem(y + k, NY)
        return remote(mid.at[lax.rem(to, REP)], recv_y.at[y], y_send.at[to], y_recv.at[y], at_y(k))

    def y_from(k):
        at = lax.rem(y + k, NY)
        return remote(mid.at[0], recv_y.at[at], y_send.at[at], y_recv.at[at], at_y(k))

    def ga_copy(k):
        src = done.at[pl.ds(0, A_Z)]
        return remote(src, gather_az.at[z], ga_send.at[k], ga_recv.at[k], at_z(k))

    def gb_copy(k):
        src = done.at[pl.ds(A_Z, B_X)]
        return remote(src, gather_bx.at[x], gb_send.at[k], gb_recv.at[k], at_x(k))

    def fa_copy(k):
        return remote(gather_az, full_a.at[core, x], fa_send.at[k], fa_recv.at[k], at_x(k))

    def fb_copy(k):
        return remote(gather_bx, full_b.at[core, z], fb_send.at[k], fb_recv.at[k], at_z(k))

    for g in range(REP // GROUP):
        lhs = pooled_sel[pl.ds(g * GROUP * HALF, GROUP * HALF), :]
        for first, width in ((0, 256), (256, 256), (512, 256), (768, 256), (1024, 128)):
            value = mm(lhs, back[:, pl.ds(first, width)]).astype(BF)
            for jj in range(width // LANE):
                j = first // LANE + jj
                for q in range(GROUP):
                    part[g * GROUP + q, pl.ds(j * HALF, HALF), :] = value[
                        q * HALF : (q + 1) * HALF, jj * LANE : (jj + 1) * LANE
                    ]
        each(NX, lambda k, g=g: ax_copy(g, k).start())
        each(NZ, lambda k, g=g: bz_copy(g, k).start())

    image_save = pltpu.make_async_copy(image_stage, image_out, loc_sem.at[4])
    text_save = pltpu.make_async_copy(text_stage, text_out, loc_sem.at[5])

    def image_gradient():
        for j in range(DIM // NTILE):
            cols = pl.ds(j * NTILE, NTILE)
            image_stage[:, cols] = mm_nt(back[own, :], head[cols, :]).astype(BF)
        image_save.start()

    def partner_images(i):
        part_rows = pl.ds(i * TOK, TOK)
        for j in range(DIM // NTILE):
            cols = pl.ds(j * NTILE, NTILE)
            direction[:, cols] = mm(pooled[part_rows, :], head[:, cols])

        def emb_rows(block):
            value = direction[block, :]
            inverse = 1.0 / jnp.sqrt(jnp.sum(value * value, axis=-1, keepdims=True) + EPS)
            rows = pl.ds(pl.multiple_of(i * TOK + block.start, 32), 32)
            image_emb[rows, :] = (value * inverse).astype(BF)

        rows_of(TOK, emb_rows)

    def text_weights():
        for j in range(3):
            rows = pl.ds(j * TOK, TOK)
            logits = scale * mm_nt(text_emb[own, :], image_emb[rows, :]) + shift
            match = idx[j].astype(F32) == row_id + own_base
            weight[:, rows] = sigmoid_weight(logits, match)

    def text_gradient():
        for j in range(DIM // NTILE):
            cols = pl.ds(j * NTILE, NTILE)
            direction[:, cols] = scale * mm(weight[...], image_emb[:, cols])

        def text_back(block):
            inverse = text_norm[block, :]
            unit = text_raw[block, :].astype(F32) * inverse
            value = direction[block, :]
            inner = jnp.sum(unit * value, axis=-1, keepdims=True)
            text_stage[block, :] = ((value - unit * inner) * inverse).astype(BF)

        rows_of(TOK, text_back)
        text_save.start()

    def first_sums(g):
        each(NX, lambda k: ax_copy(g, k).wait_recv())
        for q in range(g * GROUP, (g + 1) * GROUP):
            total = part[q, pl.ds(a_start(x), A_X), :].astype(F32)
            for k in range(1, NX):
                total = total + recv_ax[k, q].astype(F32)
            sum_ax[q] = total.astype(BF)
        each(NZ, lambda k: az_copy(g, k).start())
        each(NZ, lambda k: bz_copy(g, k).wait_recv())
        for q in range(g * GROUP, (g + 1) * GROUP):
            total = part[q, pl.ds(b_start(z), B_Z), :].astype(F32)
            for k in range(1, NZ):
                total = total + recv_bz[k, q].astype(F32)
            sum_bz[q] = total.astype(BF)
        each(NX, lambda k: bx_copy(g, k).start())

    def second_sums(g):
        group = rows_in(g)
        each(NX, lambda k: bx_copy(g, k).wait_recv())
        total = sum_bz[group, pl.ds(bx_start(x), B_X), :].astype(F32)
        for k in range(1, NX):
            total = total + recv_bx[k, group].astype(F32)
        mid[group, pl.ds(A_Z, B_X), :] = total.astype(BF)
        each(NZ, lambda k: az_copy(g, k).wait_recv())
        total = sum_ax[group, pl.ds(az_start(z), A_Z), :].astype(F32)
        for k in range(1, NZ):
            total = total + recv_az[k, group].astype(F32)
        mid[group, pl.ds(0, A_Z), :] = total.astype(BF)

        def send(k):
            @pl.when(lax.rem(y + k, REP) // GROUP == g)
            def _():
                y_copy(k).start()

        each(NY, send)

    image_gradient()
    partner_images(1)
    tasks = [
        lambda: (far_pooled.wait_recv(), partner_images(2)),
        lambda: (text_weights(), text_gradient()),
    ]
    for g in range(REP // GROUP):
        first_sums(g)
        if tasks:
            tasks.pop(0)()
    for task in tasks:
        task()
    for g in range(REP // GROUP):
        second_sums(g)

    recv_y[y] = mid[rep]
    each(NY, lambda k: y_from(k).wait_recv())
    total = recv_y[0].astype(F32)
    for k in range(1, NY):
        total = total + recv_y[k].astype(F32)
    done[...] = total.astype(BF)

    each(NX, lambda k: gb_copy(k).start())
    each(NZ, lambda k: ga_copy(k).start())
    gather_bx[x] = done[pl.ds(A_Z, B_X), :]
    gather_az[z] = done[pl.ds(0, A_Z), :]
    each(NX, lambda k: gb_copy(k).wait_recv())
    each(NZ, lambda k: fb_copy(k).start())
    each(NZ, lambda k: ga_copy(k).wait_recv())
    each(NX, lambda k: fa_copy(k).start())
    full_b[core, z] = gather_bx[...]
    full_a[core, x] = gather_az[...]
    each(NX, lambda k: fa_copy(k).wait_recv())
    each(NZ, lambda k: fb_copy(k).wait_recv())
    end_copies = [
        remote(full_a.at[core], full_a.at[core], end_send.at[0], end_recv.at[0], other),
        remote(full_b.at[core], full_b.at[core], end_send.at[1], end_recv.at[1], other),
    ]
    for copy in end_copies:
        copy.start()
    for copy in end_copies:
        copy.wait_recv()

    for half in range(2):
        for tile in range(COLS * 9):
            j, row = tile // 9, tile % 9
            if tile < A_ROWS // 16:
                place = min(tile // 15, NX - 1)
                rest = tile - min(place * 15, A_LAST // 16)
                piece = min(rest // 2, NZ - 1)
                at = rest - min(piece * 2, A_ZLAST // 16)
                value = full_a[half, place, piece, pl.ds(at * 16, 16), :]
            else:
                rest = tile - A_ROWS // 16
                value = full_b[half, rest // 3, rest % 3]
            head_stage[pl.ds(half * HALF + row * 16, 16), pl.ds(j * LANE, LANE)] = value
    head_save = pltpu.make_async_copy(head_stage, head_out, loc_sem.at[6])
    head_save.start()

    far_text.wait_send()
    far_idx.wait_send()
    far_pooled.wait_send()
    for copy in head_copies + relays + swaps + forwards + [back_copy] + end_copies:
        copy.wait_send()
    for g in range(REP // GROUP):
        for count, copy in ((NX, ax_copy), (NZ, bz_copy), (NZ, az_copy), (NX, bx_copy)):
            each(count, lambda k, copy=copy, g=g: copy(g, k).wait_send())
    for count, copy in (
        (NY, y_copy),
        (NZ, ga_copy),
        (NX, gb_copy),
        (NX, fa_copy),
        (NZ, fb_copy),
    ):
        each(count, lambda k, copy=copy: copy(k).wait_send())
    image_save.wait()
    text_save.wait()
    head_save.wait()


def body(pooled, text, head, idx, mult, shift):
    dma = pltpu.SemaphoreType.DMA
    vmem = pltpu.VMEM
    scratch = [
        vmem((3 * TOK, DIM), BF),
        vmem((3 * TOK, DIM), BF),
        vmem((3 * TOK, DIM), BF),
        vmem((3, 1, TOK), jnp.int32),
        vmem((TOK, TOK), F32),
        vmem((DIM, DIM), BF),
        vmem((DIM, 2 * TOK), BF),
        vmem((REP * HALF, 2 * TOK), BF),
        vmem((TOK, DIM), F32),
        vmem((TOK, 1), F32),
        vmem((TOK, 1), F32),
        vmem((3 * TOK, DIM), BF),
        vmem((TOK, 3 * TOK), BF),
        vmem((TOK, DIM), F32),
        vmem((2 * TOK, DIM), BF),
        vmem((REP, COLS * HALF, LANE), BF),
        vmem((NX, REP, A_X, LANE), BF),
        vmem((REP, A_X, LANE), BF),
        vmem((NZ, REP, A_Z, LANE), BF),
        vmem((NZ, REP, B_Z, LANE), BF),
        vmem((REP, B_Z, LANE), BF),
        vmem((NX, REP, B_X, LANE), BF),
        vmem((REP, A_Z + B_X, LANE), BF),
        vmem((NY, A_Z + B_X, LANE), BF),
        vmem((A_Z + B_X, LANE), BF),
        vmem((NZ, A_Z, LANE), BF),
        vmem((NX, B_X, LANE), BF),
        vmem((2, NX, NZ, A_Z, LANE), BF),
        vmem((2, NZ, NX, B_X, LANE), BF),
        vmem((TOK, DIM), BF),
        vmem((TOK, DIM), BF),
        vmem((SHARD, DIM), BF),
        dma((7,)),
    ]
    grouped = [REP // GROUP * n for n in (NX, NZ, NZ, NX)]
    for count in (3, 3, 6, 6, 1, *grouped, NY, NZ, NX, NX, NZ, 2):
        scratch += [dma((count,)), dma((count,))]
    hbm = pl.BlockSpec(memory_space=pl.ANY)
    smem = pl.BlockSpec(memory_space=pltpu.SMEM)
    image_grad, text_grad, head_grad = pl.pallas_call(
        kernel,
        out_shape=(
            jax.ShapeDtypeStruct((TOK, DIM), BF),
            jax.ShapeDtypeStruct((TOK, DIM), BF),
            jax.ShapeDtypeStruct((SHARD, DIM), BF),
        ),
        in_specs=[hbm, hbm, hbm, hbm, smem, smem],
        out_specs=(hbm, hbm, hbm),
        scratch_shapes=scratch,
        compiler_params=pltpu.CompilerParams(
            collective_id=0, has_side_effects=True, vmem_limit_bytes=56 * 2**20
        ),
        name="contrastive",
    )(pooled, text, head, idx.reshape(1, TOK), mult, shift)
    return image_grad, text_grad, head_grad.astype(F32)


def solution(mesh):
    rows = P(("dp", "rep"), None)
    in_specs = (rows, rows, P("rep", None), P(("dp", "rep")), P(), P())
    out_specs = (rows, rows, P("rep", None))
    return jax.shard_map(body, mesh=mesh, in_specs=in_specs, out_specs=out_specs, check_vma=False)
```

```python
import functools

import jax
import jax.numpy as jnp
from jax import lax
from jax.experimental import pallas as pl
from jax.experimental.pallas import tpu as pltpu
from jax.sharding import PartitionSpec as P

EPS = 1e-06
BF = jnp.bfloat16
F32 = jnp.float32
MESH = pl.DeviceIdType.MESH

NX, NY, NZ = 4, 8, 8
REP = 4
TOK = 256
DIM = 1152
LANE = 128
COLS = DIM // LANE
SHARD = DIM // REP
HALF = SHARD // 2
NTILE = 384
CHUNKS = 3
GROUP = 2

A_X = 240
A_LAST = 672
A_ROWS = 912
A_Z = 32
A_ZLAST = 208
B_Z = 48
B_X = 16
B_XN = 3


def coords():
    dp = lax.axis_index("dp")
    rep = lax.axis_index("rep")
    core = lax.rem(dp, 2)
    y_hi = lax.rem(dp // 2, 2)
    z = lax.rem(dp // 4, NZ)
    x = dp // 32
    return x, y_hi * REP + rep, z, core


def device(x, y, z, core):
    return (((x * NZ + z) * 2 + y // REP) * 2 + core, lax.rem(y, REP))


def remote(src, dst, send_sem, recv_sem, to):
    return pltpu.make_async_remote_copy(
        src_ref=src,
        dst_ref=dst,
        send_sem=send_sem,
        recv_sem=recv_sem,
        device_id=to,
        device_id_type=MESH,
    )


def each(count, step, far=False):
    def run(i, carry):
        n = i if far else count - 2 - i
        half = lax.div(n + 1, 2)
        step(count // 2 + half * (1 - 2 * lax.rem(n, 2)))
        return carry

    lax.fori_loop(0, count - 1, run, 0)


def rows_of(total, step, size=32):
    def run(i, carry):
        step(pl.ds(pl.multiple_of(i * size, size), size))
        return carry

    lax.fori_loop(0, total // size, run, 0)


def mm(a, b):
    return jnp.dot(a, b, preferred_element_type=F32)


def mm_nt(a, b):
    return lax.dot_general(a, b, (((1,), (1,)), ((), ())), preferred_element_type=F32)


def sigmoid_weight(logits, match):
    value = jax.nn.sigmoid(jnp.where(match, -logits, logits))
    return jnp.where(match, -value, value).astype(BF)


def kernel(
    pooled_in,
    text_in,
    head_in,
    idx_in,
    mult_ref,
    shift_ref,
    image_out,
    text_out,
    head_out,
    pooled,
    text_raw,
    text_emb,
    idx,
    idx_rows,
    head,
    pooled_t,
    pooled_sel,
    raw,
    norm,
    text_norm,
    image_emb,
    weight,
    direction,
    back,
    part,
    recv_ax,
    sum_ax,
    recv_az,
    recv_bz,
    sum_bz,
    recv_bx,
    mid,
    recv_y,
    done,
    gather_az,
    gather_bx,
    full_a,
    full_b,
    image_stage,
    text_stage,
    head_stage,
    loc_sem,
    swap_send,
    swap_recv,
    far_send,
    far_recv,
    head_send,
    head_recv,
    fwd_send,
    fwd_recv,
    back_send,
    back_recv,
    ax_send,
    ax_recv,
    bz_send,
    bz_recv,
    az_send,
    az_recv,
    bx_send,
    bx_recv,
    y_send,
    y_recv,
    ga_send,
    ga_recv,
    gb_send,
    gb_recv,
    fa_send,
    fa_recv,
    fb_send,
    fb_recv,
    end_send,
    end_recv,
):
    x, y, z, core = coords()
    rep = lax.rem(y, REP)
    other = device(x, y, z, 1 - core)

    def at_x(k):
        return device(lax.rem(x + k, NX), y, z, core)

    def at_y(k):
        return device(x, lax.rem(y + k, NY), z, core)

    def at_z(k):
        return device(x, y, lax.rem(z + k, NZ), core)

    far = at_x(2)

    own = pl.ds(0, TOK)
    sib = pl.ds(TOK, TOK)
    off = pl.ds(2 * TOK, TOK)
    shard_at = pl.multiple_of(rep * SHARD, 16)
    local = [
        pltpu.make_async_copy(text_in, text_raw.at[own], loc_sem.at[0]),
        pltpu.make_async_copy(pooled_in, pooled.at[own], loc_sem.at[1]),
        pltpu.make_async_copy(idx_in, idx.at[0], loc_sem.at[2]),
        pltpu.make_async_copy(head_in, head.at[pl.ds(shard_at, SHARD)], loc_sem.at[3]),
    ]
    for copy in local:
        copy.start()

    barrier = pltpu.get_barrier_semaphore()
    pl.semaphore_signal(barrier, inc=1, device_id=other, device_id_type=MESH)
    for count, at in ((NX, at_x), (NY, at_y), (NZ, at_z)):
        each(
            count,
            lambda k, at=at: pl.semaphore_signal(
                barrier, inc=1, device_id=at(k), device_id_type=MESH
            ),
        )
    pl.semaphore_wait(barrier, 1 + (NX - 1) + (NY - 1) + (NZ - 1))

    half_at = pl.multiple_of(core * HALF, 16)
    mine_at = pl.multiple_of(rep * SHARD + core * HALF, 16)
    long, short = 80, 64
    pieces = ((0, long, 1), (long, short, NY - 1), (long, short, 1), (0, long, NY - 1))
    head_copies = []
    for slot, (begin, count, step_y) in enumerate(pieces):
        head_copies.append(
            remote(
                head_in.at[pl.ds(pl.multiple_of(half_at + begin, 16), count)],
                head.at[pl.ds(pl.multiple_of(mine_at + begin, 16), count)],
                head_send.at[slot],
                head_recv.at[slot],
                at_y(step_y),
            )
        )
    far_text = remote(text_in, text_raw.at[off], far_send.at[0], far_recv.at[0], far)
    far_idx = remote(idx_in, idx.at[2], far_send.at[1], far_recv.at[1], far)
    far_pooled = remote(pooled_in, pooled.at[off], far_send.at[2], far_recv.at[2], far)
    swaps = [
        remote(text_in, text_raw.at[sib], swap_send.at[0], swap_recv.at[0], other),
        remote(pooled_in, pooled.at[sib], swap_send.at[1], swap_recv.at[1], other),
        remote(idx_in, idx.at[1], swap_send.at[2], swap_recv.at[2], other),
    ]
    far_text.start()
    for copy in head_copies:
        copy.start()
    far_idx.start()
    for copy in swaps:
        copy.start()

    scale = mult_ref[0]
    shift = shift_ref[0]

    def text_rows(start):
        def step(block):
            rows = pl.ds(pl.multiple_of(start + block.start, 32), 32)
            value = text_raw[rows, :].astype(F32)
            inverse = 1.0 / jnp.sqrt(jnp.sum(value * value, axis=-1, keepdims=True) + EPS)
            text_emb[rows, :] = (value * inverse).astype(BF)
            if start == 0:
                text_norm[block, :] = inverse

        rows_of(TOK, step)

    def turn(start):
        for j in range(COLS):
            cols = pl.ds(j * LANE, LANE)
            pooled_t[cols, pl.ds(start, TOK)] = pooled[pl.ds(start, TOK), cols].T

    local[0].wait()
    text_rows(0)
    local[1].wait()
    local[2].wait()
    turn(0)
    idx_rows[...] = jnp.broadcast_to(idx[0].astype(F32), (TOK, TOK)).T
    for copy in swaps:
        copy.wait_recv()
    text_rows(TOK)
    turn(TOK)
    for q in range(REP):
        pooled_sel[pl.ds(q * HALF, HALF), :] = pooled_t[
            pl.ds(pl.multiple_of(q * SHARD + core * HALF, 16), HALF), :
        ]
    local[3].wait()

    def rows_from(shift_y, begin, count):
        place = lax.rem(y + 2 * NY - shift_y, REP)
        return head.at[pl.ds(pl.multiple_of(place * SHARD + core * HALF + begin, 16), count)]

    forwards = []

    def forward(rows):
        slot = len(forwards)
        copy = remote(rows, rows, fwd_send.at[slot], fwd_recv.at[slot], other)
        copy.start()
        forwards.append(copy)

    relays = []
    for slot, (begin, count, step_y) in enumerate(pieces):
        head_copies[slot].wait_recv()
        rows = rows_from(step_y, begin, count)
        if slot < 2:
            relay = remote(rows, rows, head_send.at[4 + slot], head_recv.at[4 + slot], at_y(step_y))
            relay.start()
            relays.append(relay)
        forward(rows)
    for slot, (begin, count, step_y) in enumerate(pieces[:2]):
        relays[slot].wait_recv()
        forward(rows_from(2 * step_y, begin, count))

    far_text.wait_recv()
    far_pooled.start()
    far_idx.wait_recv()
    text_rows(2 * TOK)
    for copy in forwards:
        copy.wait_recv()

    for j in range(DIM // NTILE):
        cols = pl.ds(j * NTILE, NTILE)
        raw[:, cols] = mm(pooled[own, :], head[:, cols])

    def image_rows(block):
        value = raw[block, :]
        inverse = 1.0 / jnp.sqrt(jnp.sum(value * value, axis=-1, keepdims=True) + EPS)
        unit = value * inverse
        raw[block, :] = unit
        norm[block, :] = inverse
        image_emb[block, :] = unit.astype(BF)

    rows_of(TOK, image_rows)

    dp = lax.axis_index("dp")
    dp_other = dp + 1 - 2 * core
    dp_far = lax.rem(dp + 64, 128)
    lane_id = lax.broadcasted_iota(jnp.int32, (TOK, TOK), 1).astype(F32)
    row_id = lax.broadcasted_iota(jnp.int32, (TOK, TOK), 0).astype(F32)
    own_base = ((dp * REP + rep) * TOK).astype(F32)
    for j, place in enumerate((dp, dp_other, dp_far)):
        base = ((place * REP + rep) * TOK).astype(F32)
        rows = pl.ds(j * TOK, TOK)
        logits = scale * mm_nt(image_emb[own, :], text_emb[rows, :]) + shift
        weight[:, rows] = sigmoid_weight(logits, idx_rows[...] == lane_id + base)

    for j in range(DIM // NTILE):
        cols = pl.ds(j * NTILE, NTILE)
        direction[:, cols] = scale * mm(weight[...], text_emb[:, cols])

    def back_rows(block):
        unit = raw[block, :]
        value = direction[block, :]
        inner = jnp.sum(unit * value, axis=-1, keepdims=True)
        back[block, :] = ((value - unit * inner) * norm[block, :]).astype(BF)

    rows_of(TOK, back_rows)
    back_copy = remote(back.at[own], back.at[sib], back_send.at[0], back_recv.at[0], other)
    back_copy.start()
    back_copy.wait_recv()

    def rows_in(group):
        return pl.ds(group * GROUP, GROUP)

    def a_start(place):
        return pl.multiple_of(jnp.minimum(place * A_X, A_LAST), 16)

    def az_start(place):
        return pl.multiple_of(jnp.minimum(place * A_Z, A_ZLAST), 16)

    def b_start(place):
        return pl.multiple_of(A_ROWS + place * B_Z, 16)

    def bx_start(place):
        return pl.multiple_of(jnp.minimum(place, B_XN - 1) * B_X, 16)

    def ax_copy(group, k):
        src = part.at[rows_in(group), pl.ds(a_start(lax.rem(x + k, NX)), A_X), :]
        slot = group * NX + k
        dst = recv_ax.at[k, rows_in(group)]
        return remote(src, dst, ax_send.at[slot], ax_recv.at[slot], at_x(k))

    def bz_copy(group, k):
        src = part.at[rows_in(group), pl.ds(b_start(lax.rem(z + k, NZ)), B_Z), :]
        slot = group * NZ + k
        dst = recv_bz.at[k, rows_in(group)]
        return remote(src, dst, bz_send.at[slot], bz_recv.at[slot], at_z(k))

    def az_copy(group, k):
        src = sum_ax.at[rows_in(group), pl.ds(az_start(lax.rem(z + k, NZ)), A_Z), :]
        slot = group * NZ + k
        dst = recv_az.at[k, rows_in(group)]
        return remote(src, dst, az_send.at[slot], az_recv.at[slot], at_z(k))

    def bx_copy(group, k):
        src = sum_bz.at[rows_in(group), pl.ds(bx_start(lax.rem(x + k, NX)), B_X), :]
        slot = group * NX + k
        dst = recv_bx.at[k, rows_in(group)]
        return remote(src, dst, bx_send.at[slot], bx_recv.at[slot], at_x(k))

    def y_copy(k):
        to = lax.rem(y + k, NY)
        return remote(mid.at[lax.rem(to, REP)], recv_y.at[y], y_send.at[to], y_recv.at[y], at_y(k))

    def y_from(k):
        at = lax.rem(y + k, NY)
        return remote(mid.at[0], recv_y.at[at], y_send.at[at], y_recv.at[at], at_y(k))

    def ga_copy(k):
        src = done.at[pl.ds(0, A_Z)]
        return remote(src, gather_az.at[z], ga_send.at[k], ga_recv.at[k], at_z(k))

    def gb_copy(k):
        src = done.at[pl.ds(A_Z, B_X)]
        return remote(src, gather_bx.at[x], gb_send.at[k], gb_recv.at[k], at_x(k))

    def fa_copy(k):
        return remote(gather_az, full_a.at[core, x], fa_send.at[k], fa_recv.at[k], at_x(k))

    def fb_copy(k):
        src = gather_bx.at[pl.ds(0, B_XN)]
        dst = full_b.at[core, z, pl.ds(0, B_XN)]
        return remote(src, dst, fb_send.at[k], fb_recv.at[k], at_z(k))

    def pass_a(k):
        slot = lax.rem(x + NX - k, NX)
        piece = full_a.at[core, slot]
        return remote(piece, piece, end_send.at[slot], end_recv.at[slot], other)

    def pass_b(k):
        slot = lax.rem(z + NZ - k, NZ)
        piece = full_b.at[core, slot, pl.ds(0, B_XN)]
        return remote(piece, piece, end_send.at[NX + slot], end_recv.at[NX + slot], other)

    for g in range(REP // GROUP):
        lhs = pooled_sel[pl.ds(g * GROUP * HALF, GROUP * HALF), :]
        for first, width in ((0, 256), (256, 256), (512, 256), (768, 256), (1024, 128)):
            value = mm(lhs, back[:, pl.ds(first, width)]).astype(BF)
            for jj in range(width // LANE):
                j = first // LANE + jj
                for q in range(GROUP):
                    part[g * GROUP + q, pl.ds(j * HALF, HALF), :] = value[
                        q * HALF : (q + 1) * HALF, jj * LANE : (jj + 1) * LANE
                    ]
        each(NX, lambda k, g=g: ax_copy(g, k).start(), far=True)
        each(NZ, lambda k, g=g: bz_copy(g, k).start(), far=True)

    image_save = pltpu.make_async_copy(image_stage, image_out, loc_sem.at[4])
    text_save = pltpu.make_async_copy(text_stage, text_out, loc_sem.at[5])

    def image_gradient():
        for j in range(DIM // NTILE):
            cols = pl.ds(j * NTILE, NTILE)
            image_stage[:, cols] = mm_nt(back[own, :], head[cols, :]).astype(BF)
        image_save.start()

    def partner_images(i):
        part_rows = pl.ds(i * TOK, TOK)
        for j in range(DIM // NTILE):
            cols = pl.ds(j * NTILE, NTILE)
            direction[:, cols] = mm(pooled[part_rows, :], head[:, cols])

        def emb_rows(block):
            value = direction[block, :]
            inverse = 1.0 / jnp.sqrt(jnp.sum(value * value, axis=-1, keepdims=True) + EPS)
            rows = pl.ds(pl.multiple_of(i * TOK + block.start, 32), 32)
            image_emb[rows, :] = (value * inverse).astype(BF)

        rows_of(TOK, emb_rows)

    def text_weights():
        for j in range(3):
            rows = pl.ds(j * TOK, TOK)
            logits = scale * mm_nt(text_emb[own, :], image_emb[rows, :]) + shift
            match = idx[j].astype(F32) == row_id + own_base
            weight[:, rows] = sigmoid_weight(logits, match)

    def text_gradient():
        for j in range(DIM // NTILE):
            cols = pl.ds(j * NTILE, NTILE)
            direction[:, cols] = scale * mm(weight[...], image_emb[:, cols])

        def text_back(block):
            inverse = text_norm[block, :]
            unit = text_raw[block, :].astype(F32) * inverse
            value = direction[block, :]
            inner = jnp.sum(unit * value, axis=-1, keepdims=True)
            text_stage[block, :] = ((value - unit * inner) * inverse).astype(BF)

        rows_of(TOK, text_back)
        text_save.start()

    def first_sums(g):
        each(NX, lambda k: ax_copy(g, k).wait_recv())
        for q in range(g * GROUP, (g + 1) * GROUP):
            total = part[q, pl.ds(a_start(x), A_X), :].astype(F32)
            for k in range(1, NX):
                total = total + recv_ax[k, q].astype(F32)
            sum_ax[q] = total.astype(BF)
        each(NZ, lambda k: az_copy(g, k).start(), far=True)
        each(NZ, lambda k: bz_copy(g, k).wait_recv())
        for q in range(g * GROUP, (g + 1) * GROUP):
            total = part[q, pl.ds(b_start(z), B_Z), :].astype(F32)
            for k in range(1, NZ):
                total = total + recv_bz[k, q].astype(F32)
            sum_bz[q] = total.astype(BF)
        each(NX, lambda k: bx_copy(g, k).start(), far=True)

    def second_sums(g):
        group = rows_in(g)
        each(NX, lambda k: bx_copy(g, k).wait_recv())
        total = sum_bz[group, pl.ds(bx_start(x), B_X), :].astype(F32)
        for k in range(1, NX):
            total = total + recv_bx[k, group].astype(F32)
        mid[group, pl.ds(A_Z, B_X), :] = total.astype(BF)
        each(NZ, lambda k: az_copy(g, k).wait_recv())
        total = sum_ax[group, pl.ds(az_start(z), A_Z), :].astype(F32)
        for k in range(1, NZ):
            total = total + recv_az[k, group].astype(F32)
        mid[group, pl.ds(0, A_Z), :] = total.astype(BF)

        def send(k):
            @pl.when(lax.rem(y + k, REP) // GROUP == g)
            def _():
                y_copy(k).start()

        each(NY, send, far=True)

    image_gradient()
    partner_images(1)
    tasks = [
        lambda: (far_pooled.wait_recv(), partner_images(2)),
        lambda: (text_weights(), text_gradient()),
    ]
    for g in range(REP // GROUP):
        first_sums(g)
        if tasks:
            tasks.pop(0)()
    for task in tasks:
        task()
    for g in range(REP // GROUP):
        second_sums(g)

    recv_y[y] = mid[rep]
    each(NY, lambda k: y_from(k).wait_recv())
    total = recv_y[0].astype(F32)
    for k in range(1, NY):
        total = total + recv_y[k].astype(F32)
    done[...] = total.astype(BF)

    each(NX, lambda k: gb_copy(k).start(), far=True)
    each(NZ, lambda k: ga_copy(k).start(), far=True)
    gather_bx[x] = done[pl.ds(A_Z, B_X), :]
    gather_az[z] = done[pl.ds(0, A_Z), :]
    each(NX, lambda k: gb_copy(k).wait_recv())
    each(NZ, lambda k: fb_copy(k).start(), far=True)
    each(NZ, lambda k: ga_copy(k).wait_recv())
    each(NX, lambda k: fa_copy(k).start(), far=True)
    full_b[core, z] = gather_bx[...]
    pass_b(0).start()
    full_a[core, x] = gather_az[...]
    pass_a(0).start()

    def on_a(k):
        fa_copy(k).wait_recv()
        pass_a(k).start()

    def on_b(k):
        fb_copy(k).wait_recv()
        pass_b(k).start()

    each(NX, on_a)
    each(NZ, on_b)

    def place_half(half):
        base = pl.multiple_of(half * HALF, 16)
        for tile in range(COLS * 9):
            j, row = tile // 9, tile % 9
            if tile < A_ROWS // 16:
                place = min(tile // 15, NX - 1)
                rest = tile - min(place * 15, A_LAST // 16)
                piece = min(rest // 2, NZ - 1)
                at = rest - min(piece * 2, A_ZLAST // 16)
                value = full_a[half, place, piece, pl.ds(at * 16, 16), :]
            else:
                rest = tile - A_ROWS // 16
                value = full_b[half, rest // 3, rest % 3]
            head_stage[pl.ds(base + row * 16, 16), pl.ds(j * LANE, LANE)] = value

    place_half(core)
    pass_a(0).wait_recv()
    each(NX, lambda k: pass_a(k).wait_recv())
    pass_b(0).wait_recv()
    each(NZ, lambda k: pass_b(k).wait_recv())
    place_half(1 - core)
    head_save = pltpu.make_async_copy(head_stage, head_out, loc_sem.at[6])
    head_save.start()

    far_text.wait_send()
    far_idx.wait_send()
    far_pooled.wait_send()
    for copy in head_copies + relays + swaps + forwards + [back_copy, pass_a(0), pass_b(0)]:
        copy.wait_send()
    for g in range(REP // GROUP):
        for count, copy in ((NX, ax_copy), (NZ, bz_copy), (NZ, az_copy), (NX, bx_copy)):
            each(count, lambda k, copy=copy, g=g: copy(g, k).wait_send())
    for count, copy in (
        (NY, y_copy),
        (NZ, ga_copy),
        (NX, gb_copy),
        (NX, fa_copy),
        (NZ, fb_copy),
        (NX, pass_a),
        (NZ, pass_b),
    ):
        each(count, lambda k, copy=copy: copy(k).wait_send())
    image_save.wait()
    text_save.wait()
    head_save.wait()


def finish(
    image_in,
    text_in,
    head_in,
    image_out,
    text_out,
    head_out,
    image,
    text,
    narrow,
    wide,
    in_sem,
    out_sem,
    sem,
):
    size = SHARD // CHUNKS
    loads, saves = [], []
    for c in range(CHUNKS):
        rows = pl.ds(c * size, size)
        loads.append(pltpu.make_async_copy(head_in.at[rows], narrow.at[rows], in_sem.at[c]))
        saves.append(pltpu.make_async_copy(wide.at[rows], head_out.at[rows], out_sem.at[c]))
    whole = [
        (
            pltpu.make_async_copy(image_in, image, sem.at[0]),
            pltpu.make_async_copy(image, image_out, sem.at[1]),
        ),
        (
            pltpu.make_async_copy(text_in, text, sem.at[2]),
            pltpu.make_async_copy(text, text_out, sem.at[3]),
        ),
    ]
    for load in loads:
        load.start()
    for load, save in whole:
        load.start()
    for c in range(CHUNKS):
        rows = pl.ds(c * size, size)
        loads[c].wait()
        wide[rows, :] = narrow[rows, :].astype(F32)
        saves[c].start()
    for load, save in whole:
        load.wait()
        save.start()
    for save in saves:
        save.wait()
    for load, save in whole:
        save.wait()


def body(pooled, text, head, idx, mult, shift):
    dma = pltpu.SemaphoreType.DMA
    vmem = pltpu.VMEM
    scratch = [
        vmem((3 * TOK, DIM), BF),
        vmem((3 * TOK, DIM), BF),
        vmem((3 * TOK, DIM), BF),
        vmem((3, 1, TOK), jnp.int32),
        vmem((TOK, TOK), F32),
        vmem((DIM, DIM), BF),
        vmem((DIM, 2 * TOK), BF),
        vmem((REP * HALF, 2 * TOK), BF),
        vmem((TOK, DIM), F32),
        vmem((TOK, 1), F32),
        vmem((TOK, 1), F32),
        vmem((3 * TOK, DIM), BF),
        vmem((TOK, 3 * TOK), BF),
        vmem((TOK, DIM), F32),
        vmem((2 * TOK, DIM), BF),
        vmem((REP, COLS * HALF, LANE), BF),
        vmem((NX, REP, A_X, LANE), BF),
        vmem((REP, A_X, LANE), BF),
        vmem((NZ, REP, A_Z, LANE), BF),
        vmem((NZ, REP, B_Z, LANE), BF),
        vmem((REP, B_Z, LANE), BF),
        vmem((NX, REP, B_X, LANE), BF),
        vmem((REP, A_Z + B_X, LANE), BF),
        vmem((NY, A_Z + B_X, LANE), BF),
        vmem((A_Z + B_X, LANE), BF),
        vmem((NZ, A_Z, LANE), BF),
        vmem((NX, B_X, LANE), BF),
        vmem((2, NX, NZ, A_Z, LANE), BF),
        vmem((2, NZ, NX, B_X, LANE), BF),
        vmem((TOK, DIM), BF),
        vmem((TOK, DIM), BF),
        vmem((SHARD, DIM), BF),
        dma((7,)),
    ]
    grouped = [REP // GROUP * n for n in (NX, NZ, NZ, NX)]
    for count in (3, 3, 6, 6, 1, *grouped, NY, NZ, NX, NX, NZ, NX + NZ):
        scratch += [dma((count,)), dma((count,))]
    hbm = pl.BlockSpec(memory_space=pl.ANY)
    smem = pl.BlockSpec(memory_space=pltpu.SMEM)
    image_grad, text_grad, head_grad = pl.pallas_call(
        kernel,
        out_shape=(
            jax.ShapeDtypeStruct((TOK, DIM), BF),
            jax.ShapeDtypeStruct((TOK, DIM), BF),
            jax.ShapeDtypeStruct((SHARD, DIM), BF),
        ),
        in_specs=[hbm, hbm, hbm, hbm, smem, smem],
        out_specs=(hbm, hbm, hbm),
        scratch_shapes=scratch,
        compiler_params=pltpu.CompilerParams(
            collective_id=0, has_side_effects=True, vmem_limit_bytes=56 * 2**20
        ),
        name="contrastive",
    )(pooled, text, head, idx.reshape(1, TOK), mult, shift)
    hbm = pl.BlockSpec(memory_space=pltpu.HBM)
    shape = jax.ShapeDtypeStruct
    return pl.pallas_call(
        finish,
        out_shape=(shape((TOK, DIM), BF), shape((TOK, DIM), BF), shape((SHARD, DIM), F32)),
        in_specs=[hbm, hbm, hbm],
        out_specs=(hbm, hbm, hbm),
        scratch_shapes=[
            vmem((TOK, DIM), BF),
            vmem((TOK, DIM), BF),
            vmem((SHARD, DIM), BF),
            vmem((SHARD, DIM), F32),
            dma((CHUNKS,)),
            dma((CHUNKS,)),
            dma((4,)),
        ],
        compiler_params=pltpu.CompilerParams(vmem_limit_bytes=56 * 2**20),
        name="finish",
    )(image_grad, text_grad, head_grad)


def solution(mesh):
    rows = P(("dp", "rep"), None)
    in_specs = (rows, rows, P("rep", None), P(("dp", "rep")), P(), P())
    out_specs = (rows, rows, P("rep", None))
    return jax.shard_map(body, mesh=mesh, in_specs=in_specs, out_specs=out_specs, check_vma=False)
```

```python
import functools

import jax
import jax.numpy as jnp
from jax import lax
from jax.experimental import pallas as pl
from jax.experimental.pallas import tpu as pltpu
from jax.sharding import PartitionSpec as P

EPS = 1e-06
BF = jnp.bfloat16
F32 = jnp.float32
MESH = pl.DeviceIdType.MESH

NX, NY, NZ = 4, 8, 8
REP = 4
TOK = 256
DIM = 1152
LANE = 128
COLS = DIM // LANE
SHARD = DIM // REP
HALF = SHARD // 2
NTILE = 384
CHUNKS = 3
GROUP = 1

A_X = 240
A_LAST = 672
A_ROWS = 912
A_Z = 32
A_ZLAST = 208
B_Z = 48
B_X = 16
B_XN = 3


def coords():
    dp = lax.axis_index("dp")
    rep = lax.axis_index("rep")
    core = lax.rem(dp, 2)
    y_hi = lax.rem(dp // 2, 2)
    z = lax.rem(dp // 4, NZ)
    x = dp // 32
    return x, y_hi * REP + rep, z, core


def device(x, y, z, core):
    return (((x * NZ + z) * 2 + y // REP) * 2 + core, lax.rem(y, REP))


def remote(src, dst, send_sem, recv_sem, to):
    return pltpu.make_async_remote_copy(
        src_ref=src,
        dst_ref=dst,
        send_sem=send_sem,
        recv_sem=recv_sem,
        device_id=to,
        device_id_type=MESH,
    )


def each(count, step, far=False):
    def run(i, carry):
        n = i if far else count - 2 - i
        half = lax.div(n + 1, 2)
        step(count // 2 + half * (1 - 2 * lax.rem(n, 2)))
        return carry

    lax.fori_loop(0, count - 1, run, 0)


def rows_of(total, step, size=32):
    def run(i, carry):
        step(pl.ds(pl.multiple_of(i * size, size), size))
        return carry

    lax.fori_loop(0, total // size, run, 0)


def mm(a, b):
    return jnp.dot(a, b, preferred_element_type=F32)


def mm_nt(a, b):
    return lax.dot_general(a, b, (((1,), (1,)), ((), ())), preferred_element_type=F32)


def sigmoid_weight(logits, match):
    value = jax.nn.sigmoid(jnp.where(match, -logits, logits))
    return jnp.where(match, -value, value).astype(BF)


def kernel(
    pooled_in,
    text_in,
    head_in,
    idx_in,
    mult_ref,
    shift_ref,
    image_out,
    text_out,
    head_out,
    pooled,
    text_raw,
    text_emb,
    idx,
    idx_rows,
    head,
    pooled_t,
    pooled_sel,
    raw,
    norm,
    text_norm,
    image_emb,
    weight,
    direction,
    back,
    part,
    recv_ax,
    sum_ax,
    recv_az,
    recv_bz,
    sum_bz,
    recv_bx,
    mid,
    recv_y,
    done,
    gather_az,
    gather_bx,
    full_a,
    full_b,
    image_stage,
    text_stage,
    head_stage,
    loc_sem,
    swap_send,
    swap_recv,
    far_send,
    far_recv,
    head_send,
    head_recv,
    fwd_send,
    fwd_recv,
    back_send,
    back_recv,
    ax_send,
    ax_recv,
    bz_send,
    bz_recv,
    az_send,
    az_recv,
    bx_send,
    bx_recv,
    y_send,
    y_recv,
    ga_send,
    ga_recv,
    gb_send,
    gb_recv,
    fa_send,
    fa_recv,
    fb_send,
    fb_recv,
    end_send,
    end_recv,
):
    x, y, z, core = coords()
    rep = lax.rem(y, REP)
    other = device(x, y, z, 1 - core)

    def at_x(k):
        return device(lax.rem(x + k, NX), y, z, core)

    def at_y(k):
        return device(x, lax.rem(y + k, NY), z, core)

    def at_z(k):
        return device(x, y, lax.rem(z + k, NZ), core)

    far = at_x(2)

    own = pl.ds(0, TOK)
    sib = pl.ds(TOK, TOK)
    off = pl.ds(2 * TOK, TOK)
    shard_at = pl.multiple_of(rep * SHARD, 16)
    local = [
        pltpu.make_async_copy(text_in, text_raw.at[own], loc_sem.at[0]),
        pltpu.make_async_copy(pooled_in, pooled.at[own], loc_sem.at[1]),
        pltpu.make_async_copy(idx_in, idx.at[0], loc_sem.at[2]),
        pltpu.make_async_copy(head_in, head.at[pl.ds(shard_at, SHARD)], loc_sem.at[3]),
    ]
    for copy in local:
        copy.start()

    barrier = pltpu.get_barrier_semaphore()
    pl.semaphore_signal(barrier, inc=1, device_id=other, device_id_type=MESH)
    for count, at in ((NX, at_x), (NY, at_y), (NZ, at_z)):
        each(
            count,
            lambda k, at=at: pl.semaphore_signal(
                barrier, inc=1, device_id=at(k), device_id_type=MESH
            ),
        )
    pl.semaphore_wait(barrier, 1 + (NX - 1) + (NY - 1) + (NZ - 1))

    half_at = pl.multiple_of(core * HALF, 16)
    mine_at = pl.multiple_of(rep * SHARD + core * HALF, 16)
    long, short = 80, 64
    pieces = ((0, long, 1), (long, short, NY - 1), (long, short, 1), (0, long, NY - 1))
    head_copies = []
    for slot, (begin, count, step_y) in enumerate(pieces):
        head_copies.append(
            remote(
                head_in.at[pl.ds(pl.multiple_of(half_at + begin, 16), count)],
                head.at[pl.ds(pl.multiple_of(mine_at + begin, 16), count)],
                head_send.at[slot],
                head_recv.at[slot],
                at_y(step_y),
            )
        )
    far_text = remote(text_in, text_raw.at[off], far_send.at[0], far_recv.at[0], far)
    far_idx = remote(idx_in, idx.at[2], far_send.at[1], far_recv.at[1], far)
    far_pooled = remote(pooled_in, pooled.at[off], far_send.at[2], far_recv.at[2], far)
    swaps = [
        remote(text_in, text_raw.at[sib], swap_send.at[0], swap_recv.at[0], other),
        remote(pooled_in, pooled.at[sib], swap_send.at[1], swap_recv.at[1], other),
        remote(idx_in, idx.at[1], swap_send.at[2], swap_recv.at[2], other),
    ]
    far_text.start()
    for copy in head_copies:
        copy.start()
    far_idx.start()
    for copy in swaps:
        copy.start()

    scale = mult_ref[0]
    shift = shift_ref[0]

    def text_rows(start):
        def step(block):
            rows = pl.ds(pl.multiple_of(start + block.start, 32), 32)
            value = text_raw[rows, :].astype(F32)
            inverse = 1.0 / jnp.sqrt(jnp.sum(value * value, axis=-1, keepdims=True) + EPS)
            text_emb[rows, :] = (value * inverse).astype(BF)
            if start == 0:
                text_norm[block, :] = inverse

        rows_of(TOK, step)

    def turn(start):
        for j in range(COLS):
            cols = pl.ds(j * LANE, LANE)
            pooled_t[cols, pl.ds(start, TOK)] = pooled[pl.ds(start, TOK), cols].T

    local[0].wait()
    text_rows(0)
    local[1].wait()
    local[2].wait()
    turn(0)
    idx_rows[...] = jnp.broadcast_to(idx[0].astype(F32), (TOK, TOK)).T
    for copy in swaps:
        copy.wait_recv()
    text_rows(TOK)
    turn(TOK)
    for q in range(REP):
        pooled_sel[pl.ds(q * HALF, HALF), :] = pooled_t[
            pl.ds(pl.multiple_of(q * SHARD + core * HALF, 16), HALF), :
        ]
    local[3].wait()

    def rows_from(shift_y, begin, count):
        place = lax.rem(y + 2 * NY - shift_y, REP)
        return head.at[pl.ds(pl.multiple_of(place * SHARD + core * HALF + begin, 16), count)]

    forwards = []

    def forward(rows):
        slot = len(forwards)
        copy = remote(rows, rows, fwd_send.at[slot], fwd_recv.at[slot], other)
        copy.start()
        forwards.append(copy)

    relays = []
    for slot, (begin, count, step_y) in enumerate(pieces):
        head_copies[slot].wait_recv()
        rows = rows_from(step_y, begin, count)
        if slot < 2:
            relay = remote(rows, rows, head_send.at[4 + slot], head_recv.at[4 + slot], at_y(step_y))
            relay.start()
            relays.append(relay)
        forward(rows)
    for slot, (begin, count, step_y) in enumerate(pieces[:2]):
        relays[slot].wait_recv()
        forward(rows_from(2 * step_y, begin, count))

    far_text.wait_recv()
    far_pooled.start()
    far_idx.wait_recv()
    text_rows(2 * TOK)
    for copy in forwards:
        copy.wait_recv()

    for j in range(DIM // NTILE):
        cols = pl.ds(j * NTILE, NTILE)
        raw[:, cols] = mm(pooled[own, :], head[:, cols])

    def image_rows(block):
        value = raw[block, :]
        inverse = 1.0 / jnp.sqrt(jnp.sum(value * value, axis=-1, keepdims=True) + EPS)
        unit = value * inverse
        raw[block, :] = unit
        norm[block, :] = inverse
        image_emb[block, :] = unit.astype(BF)

    rows_of(TOK, image_rows)

    dp = lax.axis_index("dp")
    dp_other = dp + 1 - 2 * core
    dp_far = lax.rem(dp + 64, 128)
    lane_id = lax.broadcasted_iota(jnp.int32, (TOK, TOK), 1).astype(F32)
    row_id = lax.broadcasted_iota(jnp.int32, (TOK, TOK), 0).astype(F32)
    own_base = ((dp * REP + rep) * TOK).astype(F32)
    for j, place in enumerate((dp, dp_other, dp_far)):
        base = ((place * REP + rep) * TOK).astype(F32)
        rows = pl.ds(j * TOK, TOK)
        logits = scale * mm_nt(image_emb[own, :], text_emb[rows, :]) + shift
        weight[:, rows] = sigmoid_weight(logits, idx_rows[...] == lane_id + base)

    for j in range(DIM // NTILE):
        cols = pl.ds(j * NTILE, NTILE)
        direction[:, cols] = scale * mm(weight[...], text_emb[:, cols])

    def back_rows(block):
        unit = raw[block, :]
        value = direction[block, :]
        inner = jnp.sum(unit * value, axis=-1, keepdims=True)
        back[block, :] = ((value - unit * inner) * norm[block, :]).astype(BF)

    rows_of(TOK, back_rows)
    back_copy = remote(back.at[own], back.at[sib], back_send.at[0], back_recv.at[0], other)
    back_copy.start()
    back_copy.wait_recv()

    def rows_in(group):
        return pl.ds(group * GROUP, GROUP)

    def a_start(place):
        return pl.multiple_of(jnp.minimum(place * A_X, A_LAST), 16)

    def az_start(place):
        return pl.multiple_of(jnp.minimum(place * A_Z, A_ZLAST), 16)

    def b_start(place):
        return pl.multiple_of(A_ROWS + place * B_Z, 16)

    def bx_start(place):
        return pl.multiple_of(jnp.minimum(place, B_XN - 1) * B_X, 16)

    def ax_copy(group, k):
        src = part.at[rows_in(group), pl.ds(a_start(lax.rem(x + k, NX)), A_X), :]
        slot = group * NX + k
        dst = recv_ax.at[k, rows_in(group)]
        return remote(src, dst, ax_send.at[slot], ax_recv.at[slot], at_x(k))

    def bz_copy(group, k):
        src = part.at[rows_in(group), pl.ds(b_start(lax.rem(z + k, NZ)), B_Z), :]
        slot = group * NZ + k
        dst = recv_bz.at[k, rows_in(group)]
        return remote(src, dst, bz_send.at[slot], bz_recv.at[slot], at_z(k))

    def az_copy(group, k):
        src = sum_ax.at[rows_in(group), pl.ds(az_start(lax.rem(z + k, NZ)), A_Z), :]
        slot = group * NZ + k
        dst = recv_az.at[k, rows_in(group)]
        return remote(src, dst, az_send.at[slot], az_recv.at[slot], at_z(k))

    def bx_copy(group, k):
        src = sum_bz.at[rows_in(group), pl.ds(bx_start(lax.rem(x + k, NX)), B_X), :]
        slot = group * NX + k
        dst = recv_bx.at[k, rows_in(group)]
        return remote(src, dst, bx_send.at[slot], bx_recv.at[slot], at_x(k))

    def y_copy(k):
        to = lax.rem(y + k, NY)
        return remote(mid.at[lax.rem(to, REP)], recv_y.at[y], y_send.at[to], y_recv.at[y], at_y(k))

    def y_from(k):
        at = lax.rem(y + k, NY)
        return remote(mid.at[0], recv_y.at[at], y_send.at[at], y_recv.at[at], at_y(k))

    def ga_copy(k):
        src = done.at[pl.ds(0, A_Z)]
        return remote(src, gather_az.at[z], ga_send.at[k], ga_recv.at[k], at_z(k))

    def gb_copy(k):
        src = done.at[pl.ds(A_Z, B_X)]
        return remote(src, gather_bx.at[x], gb_send.at[k], gb_recv.at[k], at_x(k))

    def fa_copy(k):
        return remote(gather_az, full_a.at[core, x], fa_send.at[k], fa_recv.at[k], at_x(k))

    def fb_copy(k):
        src = gather_bx.at[pl.ds(0, B_XN)]
        dst = full_b.at[core, z, pl.ds(0, B_XN)]
        return remote(src, dst, fb_send.at[k], fb_recv.at[k], at_z(k))

    def pass_a(k):
        slot = lax.rem(x + NX - k, NX)
        piece = full_a.at[core, slot]
        return remote(piece, piece, end_send.at[slot], end_recv.at[slot], other)

    def pass_b(k):
        slot = lax.rem(z + NZ - k, NZ)
        piece = full_b.at[core, slot, pl.ds(0, B_XN)]
        return remote(piece, piece, end_send.at[NX + slot], end_recv.at[NX + slot], other)

    for g in range(REP // GROUP):
        lhs = pooled_sel[pl.ds(g * GROUP * HALF, GROUP * HALF), :]
        for first, width in ((0, 256), (256, 256), (512, 256), (768, 256), (1024, 128)):
            value = mm(lhs, back[:, pl.ds(first, width)]).astype(BF)
            for jj in range(width // LANE):
                j = first // LANE + jj
                for q in range(GROUP):
                    part[g * GROUP + q, pl.ds(j * HALF, HALF), :] = value[
                        q * HALF : (q + 1) * HALF, jj * LANE : (jj + 1) * LANE
                    ]
        each(NX, lambda k, g=g: ax_copy(g, k).start(), far=True)
        each(NZ, lambda k, g=g: bz_copy(g, k).start(), far=True)

    image_save = pltpu.make_async_copy(image_stage, image_out, loc_sem.at[4])
    text_save = pltpu.make_async_copy(text_stage, text_out, loc_sem.at[5])

    def image_gradient():
        for j in range(DIM // NTILE):
            cols = pl.ds(j * NTILE, NTILE)
            image_stage[:, cols] = mm_nt(back[own, :], head[cols, :]).astype(BF)
        image_save.start()

    def partner_images(i):
        part_rows = pl.ds(i * TOK, TOK)
        for j in range(DIM // NTILE):
            cols = pl.ds(j * NTILE, NTILE)
            direction[:, cols] = mm(pooled[part_rows, :], head[:, cols])

        def emb_rows(block):
            value = direction[block, :]
            inverse = 1.0 / jnp.sqrt(jnp.sum(value * value, axis=-1, keepdims=True) + EPS)
            rows = pl.ds(pl.multiple_of(i * TOK + block.start, 32), 32)
            image_emb[rows, :] = (value * inverse).astype(BF)

        rows_of(TOK, emb_rows)

    def text_weights():
        for j in range(3):
            rows = pl.ds(j * TOK, TOK)
            logits = scale * mm_nt(text_emb[own, :], image_emb[rows, :]) + shift
            match = idx[j].astype(F32) == row_id + own_base
            weight[:, rows] = sigmoid_weight(logits, match)

    def text_gradient():
        for j in range(DIM // NTILE):
            cols = pl.ds(j * NTILE, NTILE)
            direction[:, cols] = scale * mm(weight[...], image_emb[:, cols])

        def text_back(block):
            inverse = text_norm[block, :]
            unit = text_raw[block, :].astype(F32) * inverse
            value = direction[block, :]
            inner = jnp.sum(unit * value, axis=-1, keepdims=True)
            text_stage[block, :] = ((value - unit * inner) * inverse).astype(BF)

        rows_of(TOK, text_back)
        text_save.start()

    def first_sums(g):
        each(NX, lambda k: ax_copy(g, k).wait_recv())
        for q in range(g * GROUP, (g + 1) * GROUP):
            total = part[q, pl.ds(a_start(x), A_X), :].astype(F32)
            for k in range(1, NX):
                total = total + recv_ax[k, q].astype(F32)
            sum_ax[q] = total.astype(BF)
        each(NZ, lambda k: az_copy(g, k).start(), far=True)
        each(NZ, lambda k: bz_copy(g, k).wait_recv())
        for q in range(g * GROUP, (g + 1) * GROUP):
            total = part[q, pl.ds(b_start(z), B_Z), :].astype(F32)
            for k in range(1, NZ):
                total = total + recv_bz[k, q].astype(F32)
            sum_bz[q] = total.astype(BF)
        each(NX, lambda k: bx_copy(g, k).start(), far=True)

    def second_sums(g):
        group = rows_in(g)
        each(NX, lambda k: bx_copy(g, k).wait_recv())
        total = sum_bz[group, pl.ds(bx_start(x), B_X), :].astype(F32)
        for k in range(1, NX):
            total = total + recv_bx[k, group].astype(F32)
        mid[group, pl.ds(A_Z, B_X), :] = total.astype(BF)
        each(NZ, lambda k: az_copy(g, k).wait_recv())
        total = sum_ax[group, pl.ds(az_start(z), A_Z), :].astype(F32)
        for k in range(1, NZ):
            total = total + recv_az[k, group].astype(F32)
        mid[group, pl.ds(0, A_Z), :] = total.astype(BF)

        def send(k):
            @pl.when(lax.rem(y + k, REP) // GROUP == g)
            def _():
                y_copy(k).start()

        each(NY, send, far=True)

    image_gradient()
    partner_images(1)
    tasks = [
        lambda: (far_pooled.wait_recv(), partner_images(2)),
        lambda: (text_weights(), text_gradient()),
    ]
    for g in range(REP // GROUP):
        first_sums(g)
        if tasks:
            tasks.pop(0)()
    for task in tasks:
        task()
    for g in range(REP // GROUP):
        second_sums(g)

    recv_y[y] = mid[rep]
    each(NY, lambda k: y_from(k).wait_recv())
    total = recv_y[0].astype(F32)
    for k in range(1, NY):
        total = total + recv_y[k].astype(F32)
    done[...] = total.astype(BF)

    each(NX, lambda k: gb_copy(k).start(), far=True)
    each(NZ, lambda k: ga_copy(k).start(), far=True)
    gather_bx[x] = done[pl.ds(A_Z, B_X), :]
    gather_az[z] = done[pl.ds(0, A_Z), :]
    each(NX, lambda k: gb_copy(k).wait_recv())
    each(NZ, lambda k: fb_copy(k).start(), far=True)
    each(NZ, lambda k: ga_copy(k).wait_recv())
    each(NX, lambda k: fa_copy(k).start(), far=True)
    full_b[core, z] = gather_bx[...]
    pass_b(0).start()
    full_a[core, x] = gather_az[...]
    pass_a(0).start()

    def on_a(k):
        fa_copy(k).wait_recv()
        pass_a(k).start()

    def on_b(k):
        fb_copy(k).wait_recv()
        pass_b(k).start()

    each(NX, on_a)
    each(NZ, on_b)

    def place_half(half):
        base = pl.multiple_of(half * HALF, 16)
        for tile in range(COLS * 9):
            j, row = tile // 9, tile % 9
            if tile < A_ROWS // 16:
                place = min(tile // 15, NX - 1)
                rest = tile - min(place * 15, A_LAST // 16)
                piece = min(rest // 2, NZ - 1)
                at = rest - min(piece * 2, A_ZLAST // 16)
                value = full_a[half, place, piece, pl.ds(at * 16, 16), :]
            else:
                rest = tile - A_ROWS // 16
                value = full_b[half, rest // 3, rest % 3]
            head_stage[pl.ds(base + row * 16, 16), pl.ds(j * LANE, LANE)] = value

    place_half(core)
    pass_a(0).wait_recv()
    each(NX, lambda k: pass_a(k).wait_recv())
    pass_b(0).wait_recv()
    each(NZ, lambda k: pass_b(k).wait_recv())
    place_half(1 - core)
    head_save = pltpu.make_async_copy(head_stage, head_out, loc_sem.at[6])
    head_save.start()

    far_text.wait_send()
    far_idx.wait_send()
    far_pooled.wait_send()
    for copy in head_copies + relays + swaps + forwards + [back_copy, pass_a(0), pass_b(0)]:
        copy.wait_send()
    for g in range(REP // GROUP):
        for count, copy in ((NX, ax_copy), (NZ, bz_copy), (NZ, az_copy), (NX, bx_copy)):
            each(count, lambda k, copy=copy, g=g: copy(g, k).wait_send())
    for count, copy in (
        (NY, y_copy),
        (NZ, ga_copy),
        (NX, gb_copy),
        (NX, fa_copy),
        (NZ, fb_copy),
        (NX, pass_a),
        (NZ, pass_b),
    ):
        each(count, lambda k, copy=copy: copy(k).wait_send())
    image_save.wait()
    text_save.wait()
    head_save.wait()


def finish(
    image_in,
    text_in,
    head_in,
    image_out,
    text_out,
    head_out,
    image,
    text,
    narrow,
    wide,
    in_sem,
    out_sem,
    sem,
):
    size = SHARD // CHUNKS
    loads, saves = [], []
    for c in range(CHUNKS):
        rows = pl.ds(c * size, size)
        loads.append(pltpu.make_async_copy(head_in.at[rows], narrow.at[rows], in_sem.at[c]))
        saves.append(pltpu.make_async_copy(wide.at[rows], head_out.at[rows], out_sem.at[c]))
    whole = [
        (
            pltpu.make_async_copy(image_in, image, sem.at[0]),
            pltpu.make_async_copy(image, image_out, sem.at[1]),
        ),
        (
            pltpu.make_async_copy(text_in, text, sem.at[2]),
            pltpu.make_async_copy(text, text_out, sem.at[3]),
        ),
    ]
    for load in loads:
        load.start()
    for load, save in whole:
        load.start()
    for c in range(CHUNKS):
        rows = pl.ds(c * size, size)
        loads[c].wait()
        wide[rows, :] = narrow[rows, :].astype(F32)
        saves[c].start()
    for load, save in whole:
        load.wait()
        save.start()
    for save in saves:
        save.wait()
    for load, save in whole:
        save.wait()


def body(pooled, text, head, idx, mult, shift):
    dma = pltpu.SemaphoreType.DMA
    vmem = pltpu.VMEM
    scratch = [
        vmem((3 * TOK, DIM), BF),
        vmem((3 * TOK, DIM), BF),
        vmem((3 * TOK, DIM), BF),
        vmem((3, 1, TOK), jnp.int32),
        vmem((TOK, TOK), F32),
        vmem((DIM, DIM), BF),
        vmem((DIM, 2 * TOK), BF),
        vmem((REP * HALF, 2 * TOK), BF),
        vmem((TOK, DIM), F32),
        vmem((TOK, 1), F32),
        vmem((TOK, 1), F32),
        vmem((3 * TOK, DIM), BF),
        vmem((TOK, 3 * TOK), BF),
        vmem((TOK, DIM), F32),
        vmem((2 * TOK, DIM), BF),
        vmem((REP, COLS * HALF, LANE), BF),
        vmem((NX, REP, A_X, LANE), BF),
        vmem((REP, A_X, LANE), BF),
        vmem((NZ, REP, A_Z, LANE), BF),
        vmem((NZ, REP, B_Z, LANE), BF),
        vmem((REP, B_Z, LANE), BF),
        vmem((NX, REP, B_X, LANE), BF),
        vmem((REP, A_Z + B_X, LANE), BF),
        vmem((NY, A_Z + B_X, LANE), BF),
        vmem((A_Z + B_X, LANE), BF),
        vmem((NZ, A_Z, LANE), BF),
        vmem((NX, B_X, LANE), BF),
        vmem((2, NX, NZ, A_Z, LANE), BF),
        vmem((2, NZ, NX, B_X, LANE), BF),
        vmem((TOK, DIM), BF),
        vmem((TOK, DIM), BF),
        vmem((SHARD, DIM), BF),
        dma((7,)),
    ]
    grouped = [REP // GROUP * n for n in (NX, NZ, NZ, NX)]
    for count in (3, 3, 6, 6, 1, *grouped, NY, NZ, NX, NX, NZ, NX + NZ):
        scratch += [dma((count,)), dma((count,))]
    hbm = pl.BlockSpec(memory_space=pl.ANY)
    smem = pl.BlockSpec(memory_space=pltpu.SMEM)
    image_grad, text_grad, head_grad = pl.pallas_call(
        kernel,
        out_shape=(
            jax.ShapeDtypeStruct((TOK, DIM), BF),
            jax.ShapeDtypeStruct((TOK, DIM), BF),
            jax.ShapeDtypeStruct((SHARD, DIM), BF),
        ),
        in_specs=[hbm, hbm, hbm, hbm, smem, smem],
        out_specs=(hbm, hbm, hbm),
        scratch_shapes=scratch,
        compiler_params=pltpu.CompilerParams(
            collective_id=0, has_side_effects=True, vmem_limit_bytes=56 * 2**20
        ),
        name="contrastive",
    )(pooled, text, head, idx.reshape(1, TOK), mult, shift)
    hbm = pl.BlockSpec(memory_space=pltpu.HBM)
    shape = jax.ShapeDtypeStruct
    return pl.pallas_call(
        finish,
        out_shape=(shape((TOK, DIM), BF), shape((TOK, DIM), BF), shape((SHARD, DIM), F32)),
        in_specs=[hbm, hbm, hbm],
        out_specs=(hbm, hbm, hbm),
        scratch_shapes=[
            vmem((TOK, DIM), BF),
            vmem((TOK, DIM), BF),
            vmem((SHARD, DIM), BF),
            vmem((SHARD, DIM), F32),
            dma((CHUNKS,)),
            dma((CHUNKS,)),
            dma((4,)),
        ],
        compiler_params=pltpu.CompilerParams(vmem_limit_bytes=56 * 2**20),
        name="finish",
    )(image_grad, text_grad, head_grad)


def solution(mesh):
    rows = P(("dp", "rep"), None)
    in_specs = (rows, rows, P("rep", None), P(("dp", "rep")), P(), P())
    out_specs = (rows, rows, P("rep", None))
    return jax.shard_map(body, mesh=mesh, in_specs=in_specs, out_specs=out_specs, check_vma=False)
```
